128 devices in a mesh: clu: 16 (over y, x_lo, core), sta: 8 (over z, x_hi).
Axes of the slice: x: 4 (x_hi: 2, x_lo: 2; x = x_hi * 2 + x_lo), y: 4, z: 4, core: 2. Of those that a mesh axis runs over, the one named last changes fastest.
Arguments:
- waves: bfloat16 [4096, 48, 256], P('clu', 'sta'), may hold values from -1000 to 1000, as said below
- owners: int32 [4], replicated, may hold values from 0 to 15
- neighbours: int32 [16, 4], P('clu'), may hold values 0 or 1
- pair_local: int32 [16, 4, 512], P('clu'), may hold values from 0 to 63
- pair_remote: int32 [16, 4, 512], P('clu'), may hold values from 0 to 255
Outputs:
- correlation: float32 [16, 4, 65, 512], P('clu', None, None, 'sta')
The draws below stay inside these ranges and needn't reach their ends.
Inputs may be any that keep to these rules, and one draw needn't show every extreme that they name: `waves`: Real-valued waveforms.
All inputs are finite; a program needn't handle non-finite values. No bound on the sum of `neighbours` on one device may be relied on, other than what follows from the above.
Results may differ from the reference program's by a relative error of at most 0.0003.
Values may be sent and summed in bfloat16 or wider, within the bound.
No kernel may reach another device: no remote copies, remote signals or barrier semaphores. Data moves between devices by JAX's collectives and lax.ppermute only.
A program may use at most 192 MiB of HBM per device.

```python
import math
import jax
import jax.numpy as jnp
from jax import lax

CH = 48
SAMP = 256
HALF = 32
BLOCK = 64
STEPS = 4
PAIRS = 512
LAGS = 65
EV_DEV = 256
CLUSTERS = 16
EVENTS = 4096


def draw_waves(key, part):
    keys = jax.random.split(key, 5)
    template = jax.random.normal(keys[0], (CH, SAMP + 2 * HALF), jnp.float32)
    offsets = jax.random.randint(keys[1], (EVENTS,), -(HALF // 2), HALF // 2 + 1)
    index = HALF + jnp.arange(SAMP)[None, :] - offsets[:, None]
    shifted = jnp.transpose(template[:, index], (1, 0, 2))
    noise = 0.7 * jax.random.normal(keys[2], (EVENTS, CH, SAMP), jnp.float32)
    event_scale = jnp.exp(jax.random.uniform(keys[4], (EVENTS,), jnp.float32, 0.0, math.log(10.0)))
    channel_scale = jnp.exp(math.log(3.0) * jnp.arange(CH, dtype=jnp.float32) / (CH - 1) + jax.random.uniform(keys[3], (CH,), jnp.float32, 0.0, math.log(2.0)))
    values = (shifted + noise) * channel_scale[None, :, None] * event_scale[:, None, None]
    return values.astype(jnp.bfloat16)


def set_ends(drawn, own_key, least, high):
    spot = [jax.random.randint(jax.random.fold_in(own_key, axis), (), 0, length) for axis, length in enumerate(drawn.shape)]
    longest = drawn.shape.index(max(drawn.shape))
    beside = spot[:longest] + [(spot[longest] + 1) % drawn.shape[longest]] + spot[longest + 1:]
    return drawn.at[tuple(spot)].set(least).at[tuple(beside)].set(high)


def setup_inputs(seed: int = 0) -> dict:
    seeds = jax.random.split(jax.random.key(seed), 6)
    return {
        "waves": draw_waves(jax.random.fold_in(seeds[5], 71), 0),
        "owners": set_ends(jax.random.randint(seeds[1], (STEPS,), 0, CLUSTERS), jax.random.fold_in(seeds[1], 1), 0, CLUSTERS - 1).astype(jnp.int32),
        "neighbours": set_ends((jax.random.randint(seeds[2], (CLUSTERS, STEPS), 0, 4) < 3).astype(jnp.int32), jax.random.fold_in(seeds[2], 1), 0, 1),
        "pair_local": set_ends(jax.random.randint(seeds[3], (CLUSTERS, STEPS, PAIRS), 0, BLOCK), jax.random.fold_in(seeds[3], 1), 0, BLOCK - 1).astype(jnp.int32),
        "pair_remote": set_ends(jax.random.randint(seeds[4], (CLUSTERS, STEPS, PAIRS), 0, EV_DEV), jax.random.fold_in(seeds[4], 1), 0, EV_DEV - 1).astype(jnp.int32),
    }


def reference(waves, owners, neighbours, pair_local, pair_remote):
    wide = waves.astype(jnp.float32)
    energy = lax.optimization_barrier(jnp.sum(wide * wide, axis=(1, 2))) / (CH * SAMP) + 1e-06
    inv_norm = 1.0 / jnp.sqrt(energy)
    local_flat = pair_local.reshape(CLUSTERS * STEPS, PAIRS)
    remote_flat = pair_remote.reshape(CLUSTERS * STEPS, PAIRS)
    mask_flat = neighbours.reshape(CLUSTERS * STEPS).astype(jnp.float32)

    def one_group(group):
        cluster = group // STEPS
        step = group % STEPS
        local_rows = (cluster * EV_DEV + step * BLOCK + local_flat[group]).astype(jnp.int32)
        remote_rows = (owners[step] * EV_DEV + remote_flat[group]).astype(jnp.int32)
        left = wide[local_rows]
        right = wide[remote_rows]
        padded = jnp.pad(left, ((0, 0), (0, 0), (HALF, HALF)))
        values = []
        for lag_index in range(LAGS):
            start = 2 * HALF - lag_index
            values.append(lax.optimization_barrier(jnp.sum(padded[:, :, start:start + SAMP] * right, axis=(1, 2))))
        raw = jnp.stack(values, axis=0)
        factor = inv_norm[local_rows] * inv_norm[remote_rows] / (CH * SAMP) * mask_flat[group]
        return raw * factor[None, :]
    result = lax.map(one_group, jnp.arange(CLUSTERS * STEPS, dtype=jnp.int32))
    return result.reshape(CLUSTERS, STEPS, LAGS, PAIRS)
```

```python
import math

import jax
import jax.numpy as jnp
import numpy as np
from jax import lax
from jax.experimental import pallas as pl
from jax.experimental.pallas import tpu as pltpu
from jax.sharding import PartitionSpec as P

CH, SAMP, HALF, LAGS = 48, 256, 32, 65
N = 288
LO, EXTRA = 128, 17
ROWS = 72
EI, EJ = 68, 69


def tables():
    u = np.arange(SAMP)[:, None]
    k = np.arange(N // 2 + 1)[None, :]
    angle = 2 * math.pi * ((u * k) % N) / N
    c, s = np.cos(angle), np.sin(angle)
    ch, sh = c[:, LO:], s[:, LO:]
    pad = np.zeros((SAMP, 128 - 4 * EXTRA))
    left = np.concatenate([c[:, :LO], s[:, :LO], ch, sh, sh, ch, pad], axis=1)
    right = np.concatenate([c[:, :LO], s[:, :LO], ch, sh, ch, sh, pad], axis=1)
    lag = np.arange(LAGS)[:, None] - HALF
    angle = 2 * math.pi * ((lag * k) % N) / N
    weight = np.where((k == 0) | (k == N // 2), 1.0, 2.0) / N
    c, s = np.cos(angle) * weight, np.sin(angle) * weight
    back = np.zeros((ROWS, 384))
    back[:LAGS, :LO] = c[:, :LO]
    back[:LAGS, LO:2 * LO] = -s[:, :LO]
    ch, sh = c[:, LO:], s[:, LO:]
    back[:LAGS, 256:256 + 4 * EXTRA] = np.concatenate([ch, ch, -sh, sh], axis=1)
    back[LAGS, 256 + EI] = 1.0
    back[LAGS + 1, 256 + EJ] = 1.0

    def split(t, axis):
        t = t.astype(np.float32)
        hi = t.astype(jnp.bfloat16)
        lo = (t - hi.astype(np.float32)).astype(jnp.bfloat16)
        return np.concatenate([hi, lo], axis=axis)

    return split(left, 1), split(right, 1), split(back, 0)


def spectrum(x, table, energy_lane, one_lane):
    d = jnp.dot(x, table, preferred_element_type=jnp.float32)
    d = d[:, :384] + d[:, 384:]
    xf = x.astype(jnp.float32)
    energy = jnp.sum(xf * xf, axis=1, keepdims=True)
    lane = lax.broadcasted_iota(jnp.int32, (1, 128), 1)
    third = jnp.where(lane == energy_lane, energy, d[:, 256:])
    third = jnp.where(lane == one_lane, 1.0, third)
    return d[:, :128], d[:, 128:256], third


def left_kernel(w_ref, table_ref, a_ref, b_ref, c_ref):
    events = a_ref.shape[0] // 8

    def body(c, carry):
        x = w_ref[pl.ds(pl.multiple_of(c * events, events), events), :]
        parts = spectrum(x, table_ref[...], EI, EJ)
        for ref, part in zip((a_ref, b_ref, c_ref), parts):
            ref[pl.ds(c, events, stride=8), :] = part
        return carry

    lax.fori_loop(0, w_ref.shape[0] // events, body, 0)


def pair_kernel(starts, counts, channels, *refs):
    pieces = len(starts)
    base_ref, local_ref, remote_ref, la, lb, lc, table_ref, back_ref = refs[:8]
    piece_refs = refs[8:8 + pieces]
    out_ref = refs[8 + pieces]
    ra, rb, rc, tmp, z = refs[9 + pieces:]
    steps, pairs = local_ref.shape
    shares = out_ref.shape[0]
    share = pairs // shares
    block = la.shape[0] // 8 // steps
    events = la.shape[0] // 8

    for n in range(pieces):
        for m in range(counts[n]):
            step = starts[n] + m
            x = piece_refs[n][m]
            parts = spectrum(x, table_ref[...], EJ, EI)
            for g in range(x.shape[0] // 32):
                row = base_ref[n] + 32 * g
                c = row // events
                to = (row - c * events) * 8 + c + step * events * 8
                for ref, part in zip((ra, rb, rc), parts):
                    ref[pl.ds(to, 32, stride=8), :] = part[32 * g:32 * g + 32]

    for step in range(steps):

        def body(it, carry):
            for half in range(2):
                g = it * 2 + half
                for p in range(8):
                    i = pl.multiple_of((local_ref[step, g * 8 + p] + step * block) * 8, 8)
                    j = pl.multiple_of((remote_ref[step, g * 8 + p] + step * events) * 8, 8)
                    xa, xb, xc = la[pl.ds(i, 8)], lb[pl.ds(i, 8)], lc[pl.ds(i, 8)]
                    ya, yb, yc = ra[pl.ds(j, 8)], rb[pl.ds(j, 8)], rc[pl.ds(j, 8)]
                    at = half * 192 + p * 8
                    tmp[at:at + 8] = xa * ya + xb * yb
                    tmp[at + 64:at + 72] = xb * ya - xa * yb
                    tmp[at + 128:at + 136] = xc * yc
                groups = share // 8
                k = g // groups
                to = k * (steps * share) + step * share + (g - k * groups) * 8
                to = pl.multiple_of(to, 8)
                for col in range(3):
                    at = half * 192 + col * 64
                    total = tmp[pl.ds(at, 8, stride=8), :]
                    for c in range(1, channels):
                        total = total + tmp[pl.ds(at + c, 8, stride=8), :]
                    z[pl.ds(to, 8), col * 128:col * 128 + 128] = total
            return carry

        lax.fori_loop(0, pairs // 16, body, 0)

    width = steps * share
    bh, bl = back_ref[:ROWS], back_ref[ROWS:]
    contract = (((1,), (1,)), ((), ()))
    for k in range(shares):
        zk = z[k * width:(k + 1) * width]
        zh = zk.astype(jnp.bfloat16)
        zl = (zk - zh.astype(jnp.float32)).astype(jnp.bfloat16)
        dot = lambda a, b: lax.dot_general(a, b, contract, preferred_element_type=jnp.float32)
        out_ref[k] = dot(bh, zh) + dot(bh, zl) + dot(bl, zh)


def final_kernel(near_ref, r_ref, out_ref):
    total = jnp.sum(r_ref[...], axis=0)
    count = CH * SAMP
    ni = 1.0 / jnp.sqrt(total[LAGS:LAGS + 1] / count + 1e-6)
    nj = 1.0 / jnp.sqrt(total[LAGS + 1:LAGS + 2] / count + 1e-6)
    total = total[:LAGS] * (ni * nj / count)
    steps, _, share = out_ref.shape[1:]
    for s in range(steps):
        out_ref[0, s] = total[:, s * share:(s + 1) * share] * near_ref[0, s].astype(jnp.float32)


SMEM = pl.BlockSpec(memory_space=pltpu.SMEM)
VMEM = pl.BlockSpec(memory_space=pltpu.VMEM)
PARAMS = pltpu.CompilerParams(vmem_limit_bytes=48 * 1024 * 1024)


def local(waves, owners, neighbours, pair_local, pair_remote):
    ev, ch, samp = waves.shape
    steps = owners.shape[0]
    pairs = pair_local.shape[2]
    n_clu, n_sta = lax.axis_size("clu"), lax.axis_size("sta")
    share = pairs // n_sta
    left_table, right_table, back_table = (jnp.asarray(t) for t in tables())
    rows = waves.transpose(1, 0, 2).reshape(ch * ev, samp)
    chunk = ch * ev // n_clu

    f32 = jnp.float32
    plane = jax.ShapeDtypeStruct((ev * 8, 128), f32)
    la, lb, lc = pl.pallas_call(
        left_kernel, out_shape=(plane,) * 3, in_specs=[VMEM] * 2, out_specs=(VMEM,) * 3,
        compiler_params=PARAMS, name="left",
        cost_estimate=pl.CostEstimate(flops=2 * ch * ev * samp * 768, bytes_accessed=4000000, transcendentals=0),
    )(rows, left_table)

    spread = lax.all_to_all(rows.reshape(n_clu, chunk, samp), "clu", 0, 0)
    mine = jnp.stack([lax.dynamic_index_in_dim(spread, owners[s], 0, False) for s in range(steps)])

    me = lax.axis_index("clu")
    y, x, core = me // 4, me // 2 % 2, me % 2
    index = lambda y, x, c: ((y % 4) * 2 + x) * 2 + c
    flip = lambda d: [(i, i ^ d) for i in range(n_clu)]
    turn = lambda d: [(i, (i + 4 * d) % n_clu) for i in range(n_clu)]
    send = lambda v, t: lax.ppermute(v, "clu", t)
    half = steps // 2
    got = []
    for b, bx in ((mine, x), (send(mine, flip(2)), 1 - x)):
        up, down = send(b, turn(1)), send(b, turn(-1))
        got += [(b, 0, y, bx), (up, 0, y + 3, bx), (down, 0, y + 1, bx)]
        got += [(send(up[:half], turn(1)), 0, y + 2, bx), (send(down[half:], turn(-1)), half, y + 2, bx)]
    pieces, starts, bases = [], [], []
    for v, first, by, bx in got:
        for c, piece in ((core, v), (1 - core, send(v, flip(1)))):
            pieces.append(piece)
            starts.append(first)
            bases.append(index(by, bx, c) * chunk)
    counts = [p.shape[0] for p in pieces]
    base = jnp.stack(bases).astype(jnp.int32)

    def kernel(*refs):
        pair_kernel(starts, counts, ch, *refs)

    raw = pl.pallas_call(
        kernel,
        out_shape=jax.ShapeDtypeStruct((n_sta, ROWS, steps * share), f32),
        in_specs=[SMEM] * 3 + [VMEM] * (5 + len(pieces)),
        out_specs=VMEM,
        scratch_shapes=[pltpu.VMEM((steps * ev * 8, 128), f32)] * 3
        + [pltpu.VMEM((384, 128), f32), pltpu.VMEM((steps * pairs, 384), f32)],
        compiler_params=PARAMS,
        name="pairs",
    )(base, pair_local[0], pair_remote[0], la, lb, lc, right_table, back_table, *pieces)

    parts = lax.all_to_all(raw, "sta", 0, 0)
    return pl.pallas_call(
        final_kernel,
        out_shape=jax.ShapeDtypeStruct((1, steps, LAGS, share), f32),
        in_specs=[SMEM, VMEM], out_specs=VMEM, compiler_params=PARAMS, name="finish",
    )(neighbours, parts)


def solution(mesh):
    placed = (
        P("clu", "sta", None),
        P(),
        P("clu", None),
        P("clu", None, None),
        P("clu", None, None),
    )
    return jax.shard_map(
        local, mesh=mesh, in_specs=placed, out_specs=P("clu", None, None, "sta"), check_vma=False
    )
```

```python
import math

import jax
import jax.numpy as jnp
import numpy as np
from jax import lax
from jax.experimental import pallas as pl
from jax.experimental.pallas import tpu as pltpu
from jax.sharding import PartitionSpec as P

CH, SAMP, HALF, LAGS = 48, 256, 32, 65
N = 288
LO, EXTRA = 128, 17
ROWS = 72
EI, EJ = 68, 69


def tables():
    u = np.arange(SAMP)[:, None]
    k = np.arange(N // 2 + 1)[None, :]
    angle = 2 * math.pi * ((u * k) % N) / N
    c, s = np.cos(angle), np.sin(angle)
    ch, sh = c[:, LO:], s[:, LO:]
    pad = np.zeros((SAMP, 128 - 4 * EXTRA))
    left = np.concatenate([c[:, :LO], s[:, :LO], ch, sh, sh, ch, pad], axis=1)
    right = np.concatenate([c[:, :LO], s[:, :LO], ch, sh, ch, sh, pad], axis=1)
    lag = np.arange(LAGS)[:, None] - HALF
    angle = 2 * math.pi * ((lag * k) % N) / N
    weight = np.where((k == 0) | (k == N // 2), 1.0, 2.0) / N
    c, s = np.cos(angle) * weight, np.sin(angle) * weight
    back = np.zeros((ROWS, 384))
    back[:LAGS, :LO] = c[:, :LO]
    back[:LAGS, LO:2 * LO] = -s[:, :LO]
    ch, sh = c[:, LO:], s[:, LO:]
    back[:LAGS, 256:256 + 4 * EXTRA] = np.concatenate([ch, ch, -sh, sh], axis=1)
    back[LAGS, 256 + EI] = 1.0
    back[LAGS + 1, 256 + EJ] = 1.0

    def split(t, axis):
        t = t.astype(np.float32)
        hi = t.astype(jnp.bfloat16)
        lo = (t - hi.astype(np.float32)).astype(jnp.bfloat16)
        return np.concatenate([hi, lo], axis=axis)

    return split(left, 1), split(right, 1), split(back, 0)


def spectrum(x, table, energy_lane, one_lane):
    d = jnp.dot(x, table, preferred_element_type=jnp.float32)
    d = d[:, :384] + d[:, 384:]
    xf = x.astype(jnp.float32)
    energy = jnp.sum(xf * xf, axis=1, keepdims=True)
    lane = lax.broadcasted_iota(jnp.int32, (1, 128), 1)
    third = jnp.where(lane == energy_lane, energy, d[:, 256:])
    third = jnp.where(lane == one_lane, 1.0, third)
    return d[:, :128], d[:, 128:256], third


def left_kernel(table_ref, b0, b1, b2, b3, a_ref, b_ref, c_ref):
    events = a_ref.shape[0] // 8 // 4
    channels = b0.shape[0] // events
    for q, w_ref in enumerate((b0, b1, b2, b3)):
        parts = spectrum(w_ref[:channels * events], table_ref[...], EI, EJ)
        for c in range(channels):
            for ref, part in zip((a_ref, b_ref, c_ref), parts):
                ref[pl.ds(q * events * 8 + c, events, stride=8), :] = part[c * events:(c + 1) * events]


def pair_kernel(channels, base_ref, index_ref, la, lb, lc, table_ref, back_ref, p0, p1, p2, p3, out_ref, ra, rb, rc, tmp, z):
    groups4 = index_ref.shape[0]
    shares = out_ref.shape[0]
    width = out_ref.shape[2]
    share = width // groups4
    pairs = share * shares
    block = la.shape[0] // 8 // groups4
    events = ra.shape[0] // 8

    for n, p_ref in enumerate((p0, p1, p2, p3)):
        for m in range(p_ref.shape[0]):
            x = p_ref[m]
            parts = spectrum(x, table_ref[...], EJ, EI)
            for g in range(x.shape[0] // 32):
                row = base_ref[4 * n + m] + 32 * g
                c = row // events
                to = (row - c * events) * 8 + c
                for ref, part in zip((ra, rb, rc), parts):
                    ref[pl.ds(to, 32, stride=8), :] = part[32 * g:32 * g + 32]

    for q in range(groups4):

        def body(it, carry):
            for half in range(2):
                g = it * 2 + half
                for p in range(8):
                    at = g * 8 + p
                    hi, lo = at // 256, at % 256
                    i = pl.multiple_of((index_ref[q, hi, lo] + q * block) * 8, 8)
                    j = pl.multiple_of(index_ref[q, hi + pairs // 256, lo] * 8, 8)
                    xa, xb, xc = la[pl.ds(i, 8)], lb[pl.ds(i, 8)], lc[pl.ds(i, 8)]
                    ya, yb, yc = ra[pl.ds(j, 8)], rb[pl.ds(j, 8)], rc[pl.ds(j, 8)]
                    at = half * 192 + p * 8
                    tmp[at:at + 8] = xa * ya + xb * yb
                    tmp[at + 64:at + 72] = xb * ya - xa * yb
                    tmp[at + 128:at + 136] = xc * yc
                groups = share // 8
                k = g // groups
                to = k * width + q * share + (g - k * groups) * 8
                to = pl.multiple_of(to, 8)
                for col in range(3):
                    at = half * 192 + col * 64
                    total = tmp[pl.ds(at, 8, stride=8), :]
                    for c in range(1, channels):
                        total = total + tmp[pl.ds(at + c, 8, stride=8), :]
                    z[pl.ds(to, 8), col * 128:col * 128 + 128] = total
            return carry

        lax.fori_loop(0, pairs // 16, body, 0)

    bh, bl = back_ref[:ROWS], back_ref[ROWS:]
    contract = (((1,), (1,)), ((), ()))
    for k in range(shares):
        zk = z[k * width:(k + 1) * width]
        zh = zk.astype(jnp.bfloat16)
        zl = (zk - zh.astype(jnp.float32)).astype(jnp.bfloat16)
        dot = lambda a, b: lax.dot_general(a, b, contract, preferred_element_type=jnp.float32)
        out_ref[k] = dot(bh, zh) + dot(bh, zl) + dot(bl, zh)


def sum_kernel(r_ref, *out_refs):
    total = jnp.sum(r_ref[...], axis=0)
    count = CH * SAMP
    ni = 1.0 / jnp.sqrt(total[LAGS:LAGS + 1] / count + 1e-6)
    nj = 1.0 / jnp.sqrt(total[LAGS + 1:LAGS + 2] / count + 1e-6)
    total = total * (ni * nj / count)
    share = out_refs[0].shape[1]
    for q, ref in enumerate(out_refs):
        ref[...] = total[:, q * share:(q + 1) * share]


def final_kernel(step_ref, near_ref, *refs):
    out_ref = refs[-1]
    for r, ref in enumerate(refs[:-1]):
        s = step_ref[r]
        out_ref[0, s] = ref[:LAGS] * near_ref[0, s].astype(jnp.float32)


SMEM = pl.BlockSpec(memory_space=pltpu.SMEM)
VMEM = pl.BlockSpec(memory_space=pltpu.VMEM)
PARAMS = pltpu.CompilerParams(vmem_limit_bytes=48 * 1024 * 1024)


def local(waves, owners, neighbours, pair_local, pair_remote):
    ev, ch, samp = waves.shape
    steps = owners.shape[0]
    pairs = pair_local.shape[2]
    n_clu, n_sta = lax.axis_size("clu"), lax.axis_size("sta")
    share = pairs // n_sta
    block = ev // steps
    left_table, right_table, back_table = (jnp.asarray(t) for t in tables())
    cube = waves.transpose(1, 0, 2)
    rows = cube.reshape(ch * ev, samp)
    chunk = ch * ev // n_clu
    f32, bf16 = jnp.float32, jnp.bfloat16
    shaped = jax.ShapeDtypeStruct

    me = lax.axis_index("clu")
    row, step = me // 4, me % 4
    near = lambda v, d: v if d == 0 else lax.ppermute(v, "clu", [(i, i ^ d) for i in range(n_clu)])
    turn = lambda v, d: lax.ppermute(v, "clu", [(i, (i + 4 * d) % n_clu) for i in range(n_clu)])

    spread = lax.all_to_all(rows.reshape(n_clu, chunk, samp), "clu", 0, 0)
    pick = lambda d: lax.dynamic_index_in_dim(spread, owners[step ^ d], 0, False)
    mine = jnp.stack([near(pick(d), d) for d in range(4)])
    pieces = [mine, turn(mine, 1), turn(mine, -1), turn(mine, 2)]
    base = jnp.stack([((row + r) % 4 * 4 + (step ^ d)) * chunk for r in (0, 3, 1, 2) for d in range(4)])

    lists = jnp.concatenate([pair_local[0], pair_remote[0]], axis=1).astype(bf16)
    lists = lists.reshape(steps, 2 * pairs // samp, samp)
    blocks = []
    for d in range(4):
        events = lax.dynamic_slice_in_dim(cube, (step ^ d) * block, block, 1).reshape(ch * block, samp)
        listed = lax.dynamic_index_in_dim(lists, step ^ d, 0, False)
        listed = jnp.pad(listed, ((0, 16 - listed.shape[0]), (0, 0)))
        blocks.append(near(jnp.concatenate([events, listed]), d))
    index = jnp.stack([b[ch * block:ch * block + 2 * pairs // samp] for b in blocks]).astype(jnp.int32)

    plane = shaped((ev * 8, 128), f32)
    la, lb, lc = pl.pallas_call(
        left_kernel, out_shape=(plane,) * 3, in_specs=[VMEM] * 5, out_specs=(VMEM,) * 3,
        compiler_params=PARAMS, name="left",
        cost_estimate=pl.CostEstimate(flops=2 * ch * ev * samp * 768, bytes_accessed=4000000, transcendentals=0),
    )(left_table, *blocks)

    raw = pl.pallas_call(
        lambda *refs: pair_kernel(ch, *refs),
        out_shape=shaped((n_sta, ROWS, 4 * share), f32),
        in_specs=[SMEM] * 2 + [VMEM] * 9,
        out_specs=VMEM,
        scratch_shapes=[pltpu.VMEM((ev * 8, 128), f32)] * 3
        + [pltpu.VMEM((384, 128), f32), pltpu.VMEM((4 * pairs, 384), f32)],
        compiler_params=PARAMS,
        name="pairs",
    )(base, index, la, lb, lc, right_table, back_table, *pieces)

    parts = lax.all_to_all(raw, "sta", 0, 0)
    done = pl.pallas_call(
        sum_kernel, out_shape=(shaped((ROWS, share), f32),) * 4,
        in_specs=[VMEM], out_specs=(VMEM,) * 4, compiler_params=PARAMS, name="total",
    )(parts)
    done = [near(v, d) for d, v in enumerate(done)]
    order = jnp.stack([step ^ d for d in range(4)])
    return pl.pallas_call(
        final_kernel, out_shape=shaped((1, steps, LAGS, share), f32),
        in_specs=[SMEM] * 2 + [VMEM] * 4, out_specs=VMEM, compiler_params=PARAMS, name="finish",
    )(order, neighbours, *done)


def solution(mesh):
    placed = (
        P("clu", "sta", None),
        P(),
        P("clu", None),
        P("clu", None, None),
        P("clu", None, None),
    )
    return jax.shard_map(
        local, mesh=mesh, in_specs=placed, out_specs=P("clu", None, None, "sta"), check_vma=False
    )
```

```python
import math

import jax
import jax.numpy as jnp
import numpy as np
from jax import lax
from jax.experimental import pallas as pl
from jax.experimental.pallas import tpu as pltpu
from jax.sharding import PartitionSpec as P

CH, SAMP, HALF, LAGS = 48, 256, 32, 65
N = 288
LO, EXTRA = 128, 17
ROWS = 72
EI, EJ = 68, 69


def tables():
    u = np.arange(SAMP)[:, None]
    k = np.arange(N // 2 + 1)[None, :]
    angle = 2 * math.pi * ((u * k) % N) / N
    c, s = np.cos(angle), np.sin(angle)
    ch, sh = c[:, LO:], s[:, LO:]
    pad = np.zeros((SAMP, 128 - 4 * EXTRA))
    left = np.concatenate([c[:, :LO], s[:, :LO], ch, sh, sh, ch, pad], axis=1)
    right = np.concatenate([c[:, :LO], s[:, :LO], ch, sh, ch, sh, pad], axis=1)
    lag = np.arange(LAGS)[:, None] - HALF
    angle = 2 * math.pi * ((lag * k) % N) / N
    weight = np.where((k == 0) | (k == N // 2), 1.0, 2.0) / N
    c, s = np.cos(angle) * weight, np.sin(angle) * weight
    back = np.zeros((ROWS, 384))
    back[:LAGS, :LO] = c[:, :LO]
    back[:LAGS, LO:2 * LO] = -s[:, :LO]
    ch, sh = c[:, LO:], s[:, LO:]
    back[:LAGS, 256:256 + 4 * EXTRA] = np.concatenate([ch, ch, -sh, sh], axis=1)
    back[LAGS, 256 + EI] = 1.0
    back[LAGS + 1, 256 + EJ] = 1.0

    def split(t, axis):
        t = t.astype(np.float32)
        hi = t.astype(jnp.bfloat16)
        lo = (t - hi.astype(np.float32)).astype(jnp.bfloat16)
        return np.concatenate([hi, lo], axis=axis)

    return split(left, 1), split(right, 1), split(back, 0)


def spectrum(x, table, energy_lane, one_lane):
    d = jnp.dot(x, table, preferred_element_type=jnp.float32)
    d = d[:, :384] + d[:, 384:]
    xf = x.astype(jnp.float32)
    energy = jnp.sum(xf * xf, axis=1, keepdims=True)
    lane = lax.broadcasted_iota(jnp.int32, (1, 128), 1)
    third = jnp.where(lane == energy_lane, energy, d[:, 256:])
    third = jnp.where(lane == one_lane, 1.0, third)
    return d[:, :128], d[:, 128:256], third


def clear_rest(out_ref, channels):
    events = out_ref.shape[0] // 24
    for k in range(3):
        for c in range(channels, 8):
            out_ref[pl.ds(k * 8 + c, events, stride=24), :] = jnp.zeros((events, 128), jnp.float32)


def left_kernel(table_ref, b0, b1, b2, b3, out_ref):
    events = out_ref.shape[0] // 24 // 4
    channels = b0.shape[0] // events
    clear_rest(out_ref, channels)
    for q, w_ref in enumerate((b0, b1, b2, b3)):
        parts = spectrum(w_ref[:channels * events], table_ref[...], EI, EJ)
        for c in range(channels):
            for n, part in enumerate(parts):
                to = pl.ds(q * events * 24 + n * 8 + c, events, stride=24)
                out_ref[to, :] = part[c * events:(c + 1) * events]


def right_kernel(base_ref, table_ref, p0, p1, p2, p3, out_ref):
    events = out_ref.shape[0] // 24
    clear_rest(out_ref, 4 * p0.shape[0] * p0.shape[1] // events)
    for n, p_ref in enumerate((p0, p1, p2, p3)):
        for m in range(p_ref.shape[0]):
            x = p_ref[m]
            parts = spectrum(x, table_ref[...], EJ, EI)
            for g in range(x.shape[0] // 32):
                row = base_ref[4 * n + m] + 32 * g
                c = row // events
                to = (row - c * events) * 24 + c
                for k, part in enumerate(parts):
                    out_ref[pl.ds(to + 8 * k, 32, stride=24), :] = part[32 * g:32 * g + 32]


def channel_sum(vs, sub):
    for shift in (4, 2, 1):
        keep = (sub & shift) == 0
        half = len(vs) // 2
        vs = [
            jnp.where(keep, a + pltpu.roll(a, 8 - shift, 0), b + pltpu.roll(b, shift, 0))
            for a, b in zip(vs[:half], vs[half:])
        ]
    return vs[0]


def pair_kernel(order_ref, local_ref, remote_ref, left, right, back_ref, *refs):
    out_refs, z = refs[:-1], refs[-1]
    width = out_refs[0].shape[1]
    share = width // 4
    pairs = local_ref.shape[0] // 4
    bh, bl = back_ref[:ROWS], back_ref[ROWS:]
    contract = (((1,), (1,)), ((), ()))
    dot = lambda a, b: lax.dot_general(a, b, contract, preferred_element_type=jnp.float32)
    sub = lax.broadcasted_iota(jnp.int32, (8, 128), 0)
    for t, out_ref in enumerate(out_refs):
        first = order_ref[t] * share

        def body(it, carry):
            for part in range(4):
                g = it * 4 + part
                q = g >> 3
                at = q * pairs + first + (g & 7) * 8
                products = [[], [], []]
                for p in range(8):
                    i = pl.multiple_of(local_ref[at + p], 8)
                    j = pl.multiple_of(remote_ref[at + p], 8)
                    xa, xb, xc = left[pl.ds(i, 8)], left[pl.ds(i + 8, 8)], left[pl.ds(i + 16, 8)]
                    ya, yb, yc = right[pl.ds(j, 8)], right[pl.ds(j + 8, 8)], right[pl.ds(j + 16, 8)]
                    for col, v in enumerate((xa * ya + xb * yb, xb * ya - xa * yb, xc * yc)):
                        products[col].append(v)
                to = pl.multiple_of(g * 8, 8)
                for col in range(3):
                    z[pl.ds(to, 8), col * 128:col * 128 + 128] = channel_sum(products[col], sub)
            return carry

        lax.fori_loop(0, width // 32, body, 0)
        zk = z[...]
        zh = zk.astype(jnp.bfloat16)
        zl = (zk - zh.astype(jnp.float32)).astype(jnp.bfloat16)
        out_ref[...] = dot(bh, zh) + dot(bh, zl) + dot(bl, zh)


def sum_kernel(*refs):
    parts, out_refs = refs[:-4], refs[-4:]
    total = parts[0][...]
    for ref in parts[1:]:
        total = total + ref[...]
    count = CH * SAMP
    ni = 1.0 / jnp.sqrt(total[LAGS:LAGS + 1] / count + 1e-6)
    nj = 1.0 / jnp.sqrt(total[LAGS + 1:LAGS + 2] / count + 1e-6)
    total = total * (ni * nj / count)
    share = out_refs[0].shape[1]
    for q, ref in enumerate(out_refs):
        ref[...] = total[:, q * share:(q + 1) * share]


def final_kernel(step_ref, near_ref, *refs):
    out_ref = refs[-1]
    for r, ref in enumerate(refs[:-1]):
        s = step_ref[r]
        out_ref[0, s] = (ref[...] * near_ref[0, s].astype(jnp.float32)).T[:, :LAGS]


SMEM = pl.BlockSpec(memory_space=pltpu.SMEM)
VMEM = pl.BlockSpec(memory_space=pltpu.VMEM)
PARAMS = pltpu.CompilerParams(vmem_limit_bytes=48 * 1024 * 1024)


def local(waves, owners, neighbours, pair_local, pair_remote):
    ev, ch, samp = waves.shape
    steps = owners.shape[0]
    pairs = pair_local.shape[2]
    n_clu, n_sta = lax.axis_size("clu"), lax.axis_size("sta")
    share = pairs // n_sta
    block = ev // steps
    left_table, right_table, back_table = (jnp.asarray(t) for t in tables())
    cube = waves.transpose(1, 0, 2)
    rows = cube.reshape(ch * ev, samp)
    chunk = ch * ev // n_clu
    f32, bf16 = jnp.float32, jnp.bfloat16
    shaped = jax.ShapeDtypeStruct

    me = lax.axis_index("clu")
    row, step = me // 4, me % 4
    near = lambda v, d: v if d == 0 else lax.ppermute(v, "clu", [(i, i ^ d) for i in range(n_clu)])
    turn = lambda v, d: lax.ppermute(v, "clu", [(i, (i + 4 * d) % n_clu) for i in range(n_clu)])

    spread = lax.all_to_all(rows.reshape(n_clu, chunk, samp), "clu", 0, 0)
    pick = lambda d: lax.dynamic_index_in_dim(spread, owners[step ^ d], 0, False)
    mine = jnp.stack([near(pick(d), d) for d in range(4)])
    pieces = [mine, turn(mine, 1), turn(mine, -1), turn(mine, 2)]
    base = jnp.stack([((row + r) % 4 * 4 + (step ^ d)) * chunk for r in (0, 3, 1, 2) for d in range(4)])

    lists = jnp.concatenate([pair_local[0], pair_remote[0]], axis=1).astype(bf16)
    lists = lists.reshape(steps, 2 * pairs // samp, samp)
    blocks = []
    for d in range(4):
        events = lax.dynamic_slice_in_dim(cube, (step ^ d) * block, block, 1).reshape(ch * block, samp)
        listed = lax.dynamic_index_in_dim(lists, step ^ d, 0, False)
        listed = jnp.pad(listed, ((0, 16 - listed.shape[0]), (0, 0)))
        blocks.append(near(jnp.concatenate([events, listed]), d))
    listed = jnp.stack([b[ch * block:ch * block + 2 * pairs // samp] for b in blocks]).astype(jnp.int32)
    listed = listed.reshape(4, 2, pairs) * 24
    first = listed[:, 0] + jnp.arange(4, dtype=jnp.int32)[:, None] * (block * 24)
    first, second = first.reshape(4 * pairs), listed[:, 1].reshape(4 * pairs)

    spectra = shaped((ev * 24, 128), f32)
    cost = pl.CostEstimate(flops=2 * ch * ev * samp * 768, bytes_accessed=4000000, transcendentals=0)
    left = pl.pallas_call(
        left_kernel, out_shape=spectra, in_specs=[VMEM] * 5, out_specs=VMEM,
        compiler_params=PARAMS, name="left", cost_estimate=cost,
    )(left_table, *blocks)
    right = pl.pallas_call(
        right_kernel, out_shape=spectra, in_specs=[SMEM] + [VMEM] * 5, out_specs=VMEM,
        compiler_params=PARAMS, name="right", cost_estimate=cost,
    )(base, right_table, *pieces)

    sta = lax.axis_index("sta")
    moves = [(2, 1), (1, 1), (3, 1), (0, 1), (2, 0), (1, 0), (3, 0), (0, 0)]
    target = lambda k, dz, dh: ((k // 2 + dz) % (n_sta // 2)) * 2 + (k % 2 + dh) % 2
    received = []
    for some in (moves[:4], moves[4:]):
        order = jnp.stack([target(sta, *m) for m in some]).astype(jnp.int32)
        raw = pl.pallas_call(
            pair_kernel, out_shape=(shaped((ROWS, 4 * share), f32),) * len(some),
            in_specs=[SMEM] * 3 + [VMEM] * 3, out_specs=(VMEM,) * len(some),
            scratch_shapes=[pltpu.VMEM((4 * share, 384), f32)],
            compiler_params=PARAMS, name="pairs", cost_estimate=cost,
        )(order, first, second, left, right, back_table)
        for m, v in zip(some, raw):
            if m != (0, 0):
                v = lax.ppermute(v, "sta", [(k, target(k, *m)) for k in range(n_sta)])
            received.append(v)

    done = pl.pallas_call(
        sum_kernel, out_shape=(shaped((ROWS, share), f32),) * 4,
        in_specs=[VMEM] * len(received), out_specs=(VMEM,) * 4, compiler_params=PARAMS, name="total",
    )(*received)
    done = [near(v, d) for d, v in enumerate(done)]
    order = jnp.stack([step ^ d for d in range(4)])
    out = pl.pallas_call(
        final_kernel, out_shape=shaped((1, steps, share, LAGS), f32),
        in_specs=[SMEM] * 2 + [VMEM] * 4, out_specs=VMEM, compiler_params=PARAMS, name="finish",
    )(order, neighbours, *done)
    return out.transpose(0, 1, 3, 2)


def solution(mesh):
    placed = (
        P("clu", "sta", None),
        P(),
        P("clu", None),
        P("clu", None, None),
        P("clu", None, None),
    )
    return jax.shard_map(
        local, mesh=mesh, in_specs=placed, out_specs=P("clu", None, None, "sta"), check_vma=False
    )
```

```python
import math

import jax
import jax.numpy as jnp
import numpy as np
from jax import lax
from jax.experimental import pallas as pl
from jax.experimental.pallas import tpu as pltpu
from jax.sharding import PartitionSpec as P

CH, SAMP, HALF, LAGS = 48, 256, 32, 65
N = 288
LO, EXTRA = 128, 17
ROWS = 72
EI, EJ = 68, 69


def tables():
    u = np.arange(SAMP)[:, None]
    k = np.arange(N // 2 + 1)[None, :]
    angle = 2 * math.pi * ((u * k) % N) / N
    c, s = np.cos(angle), np.sin(angle)
    ch, sh = c[:, LO:], s[:, LO:]
    pad = np.zeros((SAMP, 128 - 4 * EXTRA))
    left = np.concatenate([c[:, :LO], s[:, :LO], ch, sh, sh, ch, pad], axis=1)
    right = np.concatenate([c[:, :LO], s[:, :LO], ch, sh, ch, sh, pad], axis=1)
    lag = np.arange(LAGS)[:, None] - HALF
    angle = 2 * math.pi * ((lag * k) % N) / N
    weight = np.where((k == 0) | (k == N // 2), 1.0, 2.0) / N
    c, s = np.cos(angle) * weight, np.sin(angle) * weight
    back = np.zeros((ROWS, 384))
    back[:LAGS, :LO] = c[:, :LO]
    back[:LAGS, LO:2 * LO] = -s[:, :LO]
    ch, sh = c[:, LO:], s[:, LO:]
    back[:LAGS, 256:256 + 4 * EXTRA] = np.concatenate([ch, ch, -sh, sh], axis=1)
    back[LAGS, 256 + EI] = 1.0
    back[LAGS + 1, 256 + EJ] = 1.0

    def split(t, axis):
        t = t.astype(np.float32)
        hi = t.astype(jnp.bfloat16)
        lo = (t - hi.astype(np.float32)).astype(jnp.bfloat16)
        return np.concatenate([hi, lo], axis=axis)

    return split(left, 1), split(right, 1), split(back, 0)


def spectrum(x, table, energy_lane, one_lane):
    d = jnp.dot(x, table, preferred_element_type=jnp.float32)
    d = d[:, :384] + d[:, 384:]
    xf = x.astype(jnp.float32)
    energy = jnp.sum(xf * xf, axis=1, keepdims=True)
    lane = lax.broadcasted_iota(jnp.int32, (1, 128), 1)
    third = jnp.where(lane == energy_lane, energy, d[:, 256:])
    third = jnp.where(lane == one_lane, 1.0, third)
    return d[:, :128], d[:, 128:256], third


def pick_kernel(from_ref, g0, g1, g2, g3, keep_ref, give_ref):
    for d in range(4):
        to = (keep_ref, give_ref)[d % 2]
        for n, ref in enumerate((g0, g1, g2, g3)):

            @pl.when(from_ref[d] == n)
            def _():
                to[d // 2] = ref[...]


def clear_rest(out_ref, channels):
    events = out_ref.shape[0] // 24
    for k in range(3):
        for c in range(channels, 8):
            out_ref[pl.ds(k * 8 + c, events, stride=24), :] = jnp.zeros((events, 128), jnp.float32)


def left_kernel(table_ref, b0, b1, b2, b3, out_ref):
    events = out_ref.shape[0] // 24 // 4
    channels = b0.shape[0] // events
    clear_rest(out_ref, channels)
    for q, w_ref in enumerate((b0, b1, b2, b3)):
        parts = spectrum(w_ref[:channels * events], table_ref[...], EI, EJ)
        for c in range(channels):
            for n, part in enumerate(parts):
                to = pl.ds(q * events * 24 + n * 8 + c, events, stride=24)
                out_ref[to, :] = part[c * events:(c + 1) * events]


def right_kernel(base_ref, table_ref, p0, p1, p2, p3, out_ref):
    events = out_ref.shape[0] // 24
    clear_rest(out_ref, 4 * p0.shape[0] // events)
    for n, p_ref in enumerate((p0, p1, p2, p3)):
        x = p_ref[...]
        parts = spectrum(x, table_ref[...], EJ, EI)
        for g in range(x.shape[0] // 32):
            row = base_ref[n] + 32 * g
            c = row // events
            to = (row - c * events) * 24 + c
            for k, part in enumerate(parts):
                out_ref[pl.ds(to + 8 * k, 32, stride=24), :] = part[32 * g:32 * g + 32]


def channel_sum(vs, sub):
    for shift in (4, 2, 1):
        keep = (sub & shift) == 0
        half = len(vs) // 2
        vs = [
            jnp.where(keep, a + pltpu.roll(a, 8 - shift, 0), b + pltpu.roll(b, shift, 0))
            for a, b in zip(vs[:half], vs[half:])
        ]
    return vs[0]


def pair_kernel(order_ref, local_ref, remote_ref, left, right, back_ref, out_ref, next_ref, z):
    width = out_ref.shape[2]
    half = out_ref.shape[0]
    for t in range(2 * half):
        next_ref[t] = order_ref[(t + half) % (2 * half)]
    share = width // 4
    pairs = local_ref.shape[0] // 4
    bh, bl = back_ref[:ROWS], back_ref[ROWS:]
    contract = (((1,), (1,)), ((), ()))
    dot = lambda a, b: lax.dot_general(a, b, contract, preferred_element_type=jnp.float32)
    sub = lax.broadcasted_iota(jnp.int32, (8, 128), 0)
    for t in range(half):
        first = order_ref[t] * share

        def body(it, carry):
            for part in range(4):
                g = it * 4 + part
                q = g >> 3
                at = q * pairs + first + (g & 7) * 8
                products = [[], [], []]
                for p in range(8):
                    i = pl.multiple_of(local_ref[at + p], 8)
                    j = pl.multiple_of(remote_ref[at + p], 8)
                    xa, xb, xc = left[pl.ds(i, 8)], left[pl.ds(i + 8, 8)], left[pl.ds(i + 16, 8)]
                    ya, yb, yc = right[pl.ds(j, 8)], right[pl.ds(j + 8, 8)], right[pl.ds(j + 16, 8)]
                    for col, v in enumerate((xa * ya + xb * yb, xb * ya - xa * yb, xc * yc)):
                        products[col].append(v)
                to = pl.multiple_of(g * 8, 8)
                for col in range(3):
                    z[pl.ds(to, 8), col * 128:col * 128 + 128] = channel_sum(products[col], sub)
            return carry

        lax.fori_loop(0, width // 32, body, 0)
        zk = z[...]
        zh = zk.astype(jnp.bfloat16)
        zl = (zk - zh.astype(jnp.float32)).astype(jnp.bfloat16)
        out_ref[t] = dot(bh, zh) + dot(bh, zl) + dot(bl, zh)


def add_kernel(a_ref, b_ref, *out_refs):
    for t, ref in enumerate(out_refs):
        ref[...] = a_ref[t] + b_ref[t]


def sum_kernel(*refs):
    parts, out_refs = refs[:-4], refs[-4:]
    total = parts[0][...]
    for ref in parts[1:]:
        total = total + ref[...]
    count = CH * SAMP
    ni = 1.0 / jnp.sqrt(total[LAGS:LAGS + 1] / count + 1e-6)
    nj = 1.0 / jnp.sqrt(total[LAGS + 1:LAGS + 2] / count + 1e-6)
    total = total * (ni * nj / count)
    share = out_refs[0].shape[1]
    for q, ref in enumerate(out_refs):
        ref[...] = total[:, q * share:(q + 1) * share]


def final_kernel(step_ref, near_ref, *refs):
    out_ref = refs[-1]
    for r, ref in enumerate(refs[:-1]):
        s = step_ref[r]
        out_ref[0, s] = (ref[...] * near_ref[0, s].astype(jnp.float32)).T[:, :LAGS]


SMEM = pl.BlockSpec(memory_space=pltpu.SMEM)
VMEM = pl.BlockSpec(memory_space=pltpu.VMEM)
PARAMS = pltpu.CompilerParams(vmem_limit_bytes=20 * 1024 * 1024)
SMALL = pltpu.CompilerParams(vmem_limit_bytes=8 * 1024 * 1024)


def local(waves, owners, neighbours, pair_local, pair_remote):
    ev, ch, samp = waves.shape
    steps = owners.shape[0]
    pairs = pair_local.shape[2]
    n_clu, n_sta = lax.axis_size("clu"), lax.axis_size("sta")
    share = pairs // n_sta
    block = ev // steps
    left_table, right_table, back_table = (jnp.asarray(t) for t in tables())
    cube = waves.transpose(1, 0, 2)
    rows = cube.reshape(ch * ev, samp)
    f32, bf16 = jnp.float32, jnp.bfloat16
    shaped = jax.ShapeDtypeStruct

    me = lax.axis_index("clu")
    row, step = me // 4, me % 4
    near = lambda v, d: v if d == 0 else lax.ppermute(v, "clu", [(i, i ^ d) for i in range(n_clu)])
    turn = lambda v, d: lax.ppermute(v, "clu", [(i, (i + 4 * d) % n_clu) for i in range(n_clu)])

    quarter = ch * ev // 4
    got = []
    for d in range(4):
        part = lax.dynamic_slice_in_dim(rows, (row + d) % 4 * quarter, quarter, 0)
        got.append(part if d == 0 else turn(part, d))
    source = [owners[step ^ d] for d in range(4)]
    keep, give = pl.pallas_call(
        pick_kernel, out_shape=(shaped((2, quarter, samp), bf16),) * 2,
        in_specs=[SMEM] + [VMEM] * 4, out_specs=(VMEM,) * 2, compiler_params=SMALL, name="pick",
    )(jnp.stack([(row + 4 - o // 4) % 4 for o in source]), *got)
    other = near(give, 1)
    mine = jnp.where(source[0] % 2 == me % 2, keep[0], other[0])
    theirs = jnp.where(source[2] % 2 == me % 2, keep[1], other[1])
    mine = jnp.where(source[0] // 2 % 2 == me // 2 % 2, mine, near(theirs, 2))
    pieces = [mine] + [turn(mine, d) for d in (1, -1, 2)]
    base = jnp.stack([(row + r) % 4 * quarter for r in (0, 3, 1, 2)])

    lists = jnp.concatenate([pair_local[0], pair_remote[0]], axis=1).astype(bf16)
    lists = lists.reshape(steps, 2 * pairs // samp, samp)
    blocks = []
    for d in range(4):
        events = lax.dynamic_slice_in_dim(cube, (step ^ d) * block, block, 1).reshape(ch * block, samp)
        listed = lax.dynamic_index_in_dim(lists, step ^ d, 0, False)
        listed = jnp.pad(listed, ((0, 16 - listed.shape[0]), (0, 0)))
        blocks.append(near(jnp.concatenate([events, listed]), d))
    listed = jnp.stack([b[ch * block:ch * block + 2 * pairs // samp] for b in blocks]).astype(jnp.int32)
    listed = listed.reshape(4, 2, pairs) * 24
    first = listed[:, 0] + jnp.arange(4, dtype=jnp.int32)[:, None] * (block * 24)
    first, second = first.reshape(4 * pairs), listed[:, 1].reshape(4 * pairs)

    spectra = shaped((ev * 24, 128), f32)
    cost = pl.CostEstimate(flops=2 * ch * ev * samp * 768, bytes_accessed=4000000, transcendentals=0)
    left = pl.pallas_call(
        left_kernel, out_shape=spectra, in_specs=[VMEM] * 5, out_specs=VMEM,
        compiler_params=PARAMS, name="left", cost_estimate=cost,
    )(left_table, *blocks)
    right = pl.pallas_call(
        right_kernel, out_shape=spectra, in_specs=[SMEM] + [VMEM] * 5, out_specs=VMEM,
        compiler_params=PARAMS, name="right", cost_estimate=cost,
    )(base, right_table, *pieces)

    sta = lax.axis_index("sta")
    moves = (2, 1, 3, 0)
    target = lambda k, dz, dh: ((k // 2 + dz) % (n_sta // 2)) * 2 + (k % 2 + dh) % 2
    order = jnp.stack([target(sta, dz, dh) for dh in (1, 0) for dz in moves]).astype(jnp.int32)
    halves = []
    for _ in range(2):
        raw, order = pl.pallas_call(
            pair_kernel,
            out_shape=(shaped((n_sta // 2, ROWS, 4 * share), f32), shaped((n_sta,), jnp.int32)),
            in_specs=[SMEM] * 3 + [VMEM] * 3, out_specs=(VMEM, SMEM),
            scratch_shapes=[pltpu.VMEM((4 * share, 384), f32)],
            compiler_params=PARAMS, name="pairs", cost_estimate=cost,
        )(order, first, second, left, right, back_table)
        halves.append(raw)
    across = lax.ppermute(halves[0], "sta", [(k, target(k, 0, 1)) for k in range(n_sta)])
    sums = pl.pallas_call(
        add_kernel, out_shape=(shaped((ROWS, 4 * share), f32),) * 4,
        in_specs=[VMEM] * 2, out_specs=(VMEM,) * 4, compiler_params=SMALL, name="add",
    )(across, halves[1])
    received = [
        v if dz == 0 else lax.ppermute(v, "sta", [(k, target(k, dz, 0)) for k in range(n_sta)])
        for dz, v in zip(moves, sums)
    ]

    done = pl.pallas_call(
        sum_kernel, out_shape=(shaped((ROWS, share), f32),) * 4,
        in_specs=[VMEM] * len(received), out_specs=(VMEM,) * 4, compiler_params=SMALL, name="total",
    )(*received)
    done = [near(v, d) for d, v in enumerate(done)]
    order = jnp.stack([step ^ d for d in range(4)])
    out = pl.pallas_call(
        final_kernel, out_shape=shaped((1, steps, share, LAGS), f32),
        in_specs=[SMEM] * 2 + [VMEM] * 4, out_specs=VMEM, compiler_params=PARAMS, name="finish",
    )(order, neighbours, *done)
    return out.transpose(0, 1, 3, 2)


def solution(mesh):
    placed = (
        P("clu", "sta", None),
        P(),
        P("clu", None),
        P("clu", None, None),
        P("clu", None, None),
    )
    return jax.shard_map(
        local, mesh=mesh, in_specs=placed, out_specs=P("clu", None, None, "sta"), check_vma=False
    )
```

```python
import functools
import math

import jax
import jax.numpy as jnp
import numpy as np
from jax import lax
from jax.experimental import pallas as pl
from jax.experimental.pallas import tpu as pltpu
from jax.sharding import PartitionSpec as P

CH, SAMP, HALF, LAGS = 48, 256, 32, 65
N = 288
LO, EXTRA = 128, 17
ROWS = 72
EI, EJ = 68, 69


def tables():
    u = np.arange(SAMP)[:, None]
    k = np.arange(N // 2 + 1)[None, :]
    angle = 2 * math.pi * ((u * k) % N) / N
    c, s = np.cos(angle), np.sin(angle)
    ch, sh = c[:, LO:], s[:, LO:]
    pad = np.zeros((SAMP, 128 - 4 * EXTRA))
    left = np.concatenate([c[:, :LO], s[:, :LO], ch, sh, sh, ch, pad], axis=1)
    right = np.concatenate([c[:, :LO], s[:, :LO], ch, sh, ch, sh, pad], axis=1)
    lag = np.arange(LAGS)[:, None] - HALF
    angle = 2 * math.pi * ((lag * k) % N) / N
    weight = np.where((k == 0) | (k == N // 2), 1.0, 2.0) / N
    c, s = np.cos(angle) * weight, np.sin(angle) * weight
    back = np.zeros((ROWS, 384))
    back[:LAGS, :LO] = c[:, :LO]
    back[:LAGS, LO:2 * LO] = -s[:, :LO]
    ch, sh = c[:, LO:], s[:, LO:]
    back[:LAGS, 256:256 + 4 * EXTRA] = np.concatenate([ch, ch, -sh, sh], axis=1)
    back[LAGS, 256 + EI] = 1.0
    back[LAGS + 1, 256 + EJ] = 1.0

    def split(t, axis):
        t = t.astype(np.float32)
        hi = t.astype(jnp.bfloat16)
        lo = (t - hi.astype(np.float32)).astype(jnp.bfloat16)
        return np.concatenate([hi, lo], axis=axis)

    return split(left, 1), split(right, 1), split(back, 0)


def spectrum(x, table, energy_lane, one_lane):
    d = jnp.dot(x, table, preferred_element_type=jnp.float32)
    d = d[:, :384] + d[:, 384:]
    xf = x.astype(jnp.float32)
    energy = jnp.sum(xf * xf, axis=1, keepdims=True)
    lane = lax.broadcasted_iota(jnp.int32, (1, 128), 1)
    third = jnp.where(lane == energy_lane, energy, d[:, 256:])
    third = jnp.where(lane == one_lane, 1.0, third)
    return d[:, :128], d[:, 128:256], third


def place():
    me = lax.axis_index("clu")
    return me >> 2, me & 3, (me >> 1) & 1, me & 1


def pick_kernel(owners_ref, g0, g1, g2, g3, keep_ref, give_ref):
    row, step, _, _ = place()
    for d in range(4):
        to = (keep_ref, give_ref)[d % 2]
        behind = (row + 4 - (owners_ref[step ^ d] >> 2)) & 3
        for n, ref in enumerate((g0, g1, g2, g3)):

            @pl.when(behind == n)
            def _():
                to[d // 2] = ref[...]


def core_kernel(owners_ref, kept_ref, got_ref, mine_ref, theirs_ref):
    _, step, _, core = place()
    for d, to in ((0, mine_ref), (2, theirs_ref)):
        here = (owners_ref[step ^ d] & 1) == core

        @pl.when(here)
        def _():
            to[...] = kept_ref[d // 2]

        @pl.when(jnp.logical_not(here))
        def _():
            to[...] = got_ref[d // 2]


def chip_kernel(owners_ref, mine_ref, got_ref, out_ref):
    _, step, x, _ = place()
    here = ((owners_ref[step] >> 1) & 1) == x

    @pl.when(here)
    def _():
        out_ref[...] = mine_ref[...]

    @pl.when(jnp.logical_not(here))
    def _():
        out_ref[...] = got_ref[...]


def clear_rest(out_ref, channels):
    events = out_ref.shape[0] // 24
    for k in range(3):
        for c in range(channels, 8):
            out_ref[pl.ds(k * 8 + c, events, stride=24), :] = jnp.zeros((events, 128), jnp.float32)


def left_kernel(table_ref, b0, b1, b2, b3, out_ref):
    events = out_ref.shape[0] // 24 // 4
    channels = b0.shape[0] // events
    clear_rest(out_ref, channels)
    for q, w_ref in enumerate((b0, b1, b2, b3)):
        parts = spectrum(w_ref[:channels * events], table_ref[...], EI, EJ)
        for c in range(channels):
            for n, part in enumerate(parts):
                to = pl.ds(q * events * 24 + n * 8 + c, events, stride=24)
                out_ref[to, :] = part[c * events:(c + 1) * events]


def right_kernel(table_ref, p0, p1, p2, p3, out_ref):
    events = out_ref.shape[0] // 24
    clear_rest(out_ref, 4 * p0.shape[0] // events)
    row = place()[0]
    for behind, p_ref in ((0, p0), (1, p1), (3, p2), (2, p3)):
        base = ((row + 4 - behind) & 3) * p_ref.shape[0]
        x = p_ref[...]
        parts = spectrum(x, table_ref[...], EJ, EI)
        for g in range(x.shape[0] // 32):
            at = base + 32 * g
            c = at // events
            to = (at - c * events) * 24 + c
            for k, part in enumerate(parts):
                out_ref[pl.ds(to + 8 * k, 32, stride=24), :] = part[32 * g:32 * g + 32]


def channel_sum(vs, sub):
    for shift in (4, 2, 1):
        keep = (sub & shift) == 0
        half = len(vs) // 2
        vs = [
            jnp.where(keep, a + pltpu.roll(a, 8 - shift, 0), b + pltpu.roll(b, shift, 0))
            for a, b in zip(vs[:half], vs[half:])
        ]
    return vs[0]


MOVES = (2, 1, 3, 0)


def target(k, dz, dh, count):
    return ((k // 2 + dz) % (count // 2)) * 2 + (k % 2 + dh) % 2


def pair_kernel(across, token_ref, local_ref, remote_ref, left, right, back_ref, out_ref, next_ref, z):
    width = out_ref.shape[2]
    half = out_ref.shape[0]
    next_ref[0] = token_ref[0]
    sta = lax.axis_index("sta")
    share = width // 4
    pairs = local_ref.shape[0] // 4
    bh, bl = back_ref[:ROWS], back_ref[ROWS:]
    contract = (((1,), (1,)), ((), ()))
    dot = lambda a, b: lax.dot_general(a, b, contract, preferred_element_type=jnp.float32)
    sub = lax.broadcasted_iota(jnp.int32, (8, 128), 0)
    for t in range(half):
        first = target(sta, MOVES[t], across, 2 * half) * share

        def body(it, carry):
            for part in range(4):
                g = it * 4 + part
                q = g >> 3
                at = q * pairs + first + (g & 7) * 8
                products = [[], [], []]
                for p in range(8):
                    i = pl.multiple_of(local_ref[at + p], 8)
                    j = pl.multiple_of(remote_ref[at + p], 8)
                    xa, xb, xc = left[pl.ds(i, 8)], left[pl.ds(i + 8, 8)], left[pl.ds(i + 16, 8)]
                    ya, yb, yc = right[pl.ds(j, 8)], right[pl.ds(j + 8, 8)], right[pl.ds(j + 16, 8)]
                    for col, v in enumerate((xa * ya + xb * yb, xb * ya - xa * yb, xc * yc)):
                        products[col].append(v)
                to = pl.multiple_of(g * 8, 8)
                for col in range(3):
                    z[pl.ds(to, 8), col * 128:col * 128 + 128] = channel_sum(products[col], sub)
            return carry

        lax.fori_loop(0, width // 32, body, 0)
        zk = z[...]
        zh = zk.astype(jnp.bfloat16)
        zl = (zk - zh.astype(jnp.float32)).astype(jnp.bfloat16)
        out_ref[t] = dot(bh, zh) + dot(bh, zl) + dot(bl, zh)


def add_kernel(a_ref, b_ref, *out_refs):
    for t, ref in enumerate(out_refs):
        ref[...] = a_ref[t] + b_ref[t]


def sum_kernel(*refs):
    parts, out_refs = refs[:-4], refs[-4:]
    total = parts[0][...]
    for ref in parts[1:]:
        total = total + ref[...]
    count = CH * SAMP
    ni = 1.0 / jnp.sqrt(total[LAGS:LAGS + 1] / count + 1e-6)
    nj = 1.0 / jnp.sqrt(total[LAGS + 1:LAGS + 2] / count + 1e-6)
    total = total * (ni * nj / count)
    share = out_refs[0].shape[1]
    for q, ref in enumerate(out_refs):
        ref[...] = total[:, q * share:(q + 1) * share]


def final_kernel(near_ref, *refs):
    out_ref = refs[-1]
    step = place()[1]
    for r, ref in enumerate(refs[:-1]):
        s = step ^ r
        out_ref[0, s] = (ref[...] * near_ref[0, s].astype(jnp.float32)).T[:, :LAGS]


SMEM = pl.BlockSpec(memory_space=pltpu.SMEM)
VMEM = pl.BlockSpec(memory_space=pltpu.VMEM)
PARAMS = pltpu.CompilerParams(vmem_limit_bytes=20 * 1024 * 1024)
SMALL = pltpu.CompilerParams(vmem_limit_bytes=8 * 1024 * 1024)


def local(waves, owners, neighbours, pair_local, pair_remote):
    ev, ch, samp = waves.shape
    steps = owners.shape[0]
    pairs = pair_local.shape[2]
    n_clu, n_sta = lax.axis_size("clu"), lax.axis_size("sta")
    share = pairs // n_sta
    block = ev // steps
    left_table, right_table, back_table = (jnp.asarray(t) for t in tables())
    cube = waves.transpose(1, 0, 2)
    rows = cube.reshape(ch * ev, samp)
    f32, bf16 = jnp.float32, jnp.bfloat16
    shaped = jax.ShapeDtypeStruct

    me = lax.axis_index("clu")
    row, step = me // 4, me % 4
    near = lambda v, d: v if d == 0 else lax.ppermute(v, "clu", [(i, i ^ d) for i in range(n_clu)])
    turn = lambda v, d: lax.ppermute(v, "clu", [(i, (i + 4 * d) % n_clu) for i in range(n_clu)])

    quarter = ch * ev // 4
    got = []
    for d in range(4):
        part = lax.dynamic_slice_in_dim(rows, (row + d) % 4 * quarter, quarter, 0)
        got.append(part if d == 0 else turn(part, d))
    piece = shaped((quarter, samp), bf16)
    two = shaped((2, quarter, samp), bf16)
    keep, give = pl.pallas_call(
        pick_kernel, out_shape=(two, two), in_specs=[SMEM] + [VMEM] * 4, out_specs=(VMEM,) * 2,
        compiler_params=SMALL, name="pick",
    )(owners, *got)
    mine, theirs = pl.pallas_call(
        core_kernel, out_shape=(piece, piece), in_specs=[SMEM] + [VMEM] * 2, out_specs=(VMEM,) * 2,
        compiler_params=SMALL, name="over_core",
    )(owners, keep, near(give, 1))
    mine = pl.pallas_call(
        chip_kernel, out_shape=piece, in_specs=[SMEM] + [VMEM] * 2, out_specs=VMEM,
        compiler_params=SMALL, name="over_x",
    )(owners, mine, near(theirs, 2))
    pieces = [mine] + [turn(mine, d) for d in (1, -1, 2)]

    lists = jnp.concatenate([pair_local[0], pair_remote[0]], axis=1).astype(bf16)
    lists = lists.reshape(steps, 2 * pairs // samp, samp)
    blocks = []
    for d in range(4):
        events = lax.dynamic_slice_in_dim(cube, (step ^ d) * block, block, 1).reshape(ch * block, samp)
        listed = lax.dynamic_index_in_dim(lists, step ^ d, 0, False)
        listed = jnp.pad(listed, ((0, 16 - listed.shape[0]), (0, 0)))
        blocks.append(near(jnp.concatenate([events, listed]), d))
    listed = jnp.stack([b[ch * block:ch * block + 2 * pairs // samp] for b in blocks]).astype(jnp.int32)
    listed = listed.reshape(4, 2, pairs) * 24
    first = listed[:, 0] + jnp.arange(4, dtype=jnp.int32)[:, None] * (block * 24)
    first, second = first.reshape(4 * pairs), listed[:, 1].reshape(4 * pairs)

    spectra = shaped((ev * 24, 128), f32)
    cost = pl.CostEstimate(flops=2 * ch * ev * samp * 768, bytes_accessed=4000000, transcendentals=0)
    left = pl.pallas_call(
        left_kernel, out_shape=spectra, in_specs=[VMEM] * 5, out_specs=VMEM,
        compiler_params=PARAMS, name="left", cost_estimate=cost,
    )(left_table, *blocks)
    right = pl.pallas_call(
        right_kernel, out_shape=spectra, in_specs=[VMEM] * 5, out_specs=VMEM,
        compiler_params=PARAMS, name="right", cost_estimate=cost,
    )(right_table, *pieces)

    halves = []
    token = owners
    for across in (1, 0):
        raw, token = pl.pallas_call(
            functools.partial(pair_kernel, across),
            out_shape=(shaped((n_sta // 2, ROWS, 4 * share), f32), shaped((steps,), jnp.int32)),
            in_specs=[SMEM] * 3 + [VMEM] * 3, out_specs=(VMEM, SMEM),
            scratch_shapes=[pltpu.VMEM((4 * share, 384), f32)],
            compiler_params=PARAMS, name="pairs", cost_estimate=cost,
        )(token, first, second, left, right, back_table)
        halves.append(raw)
    hop = lambda v, dz, dh: lax.ppermute(v, "sta", [(k, target(k, dz, dh, n_sta)) for k in range(n_sta)])
    sums = pl.pallas_call(
        add_kernel, out_shape=(shaped((ROWS, 4 * share), f32),) * 4,
        in_specs=[VMEM] * 2, out_specs=(VMEM,) * 4, compiler_params=SMALL, name="add",
    )(hop(halves[0], 0, 1), halves[1])
    received = [v if dz == 0 else hop(v, dz, 0) for dz, v in zip(MOVES, sums)]

    done = pl.pallas_call(
        sum_kernel, out_shape=(shaped((ROWS, share), f32),) * 4,
        in_specs=[VMEM] * len(received), out_specs=(VMEM,) * 4, compiler_params=SMALL, name="total",
    )(*received)
    done = [near(v, d) for d, v in enumerate(done)]
    out = pl.pallas_call(
        final_kernel, out_shape=shaped((1, steps, share, LAGS), f32),
        in_specs=[SMEM] + [VMEM] * 4, out_specs=VMEM, compiler_params=SMALL, name="finish",
    )(neighbours, *done)
    return out.transpose(0, 1, 3, 2)


def solution(mesh):
    placed = (
        P("clu", "sta", None),
        P(),
        P("clu", None),
        P("clu", None, None),
        P("clu", None, None),
    )
    return jax.shard_map(
        local, mesh=mesh, in_specs=placed, out_specs=P("clu", None, None, "sta"), check_vma=False
    )
```

```python
import functools
import math

import jax
import jax.numpy as jnp
import numpy as np
from jax import lax
from jax.experimental import pallas as pl
from jax.experimental.pallas import tpu as pltpu
from jax.sharding import PartitionSpec as P

CH, SAMP, HALF, LAGS = 48, 256, 32, 65
N = 288
LO, EXTRA = 128, 17
ROWS = 72
EI, EJ = 68, 69


def tables():
    u = np.arange(SAMP)[:, None]
    k = np.arange(N // 2 + 1)[None, :]
    angle = 2 * math.pi * ((u * k) % N) / N
    c, s = np.cos(angle), np.sin(angle)
    ch, sh = c[:, LO:], s[:, LO:]
    pad = np.zeros((SAMP, 128 - 4 * EXTRA))
    left = np.concatenate([c[:, :LO], s[:, :LO], ch, sh, sh, ch, pad], axis=1)
    right = np.concatenate([c[:, :LO], s[:, :LO], ch, sh, ch, sh, pad], axis=1)
    lag = np.arange(LAGS)[:, None] - HALF
    angle = 2 * math.pi * ((lag * k) % N) / N
    weight = np.where((k == 0) | (k == N // 2), 1.0, 2.0) / N
    c, s = np.cos(angle) * weight, np.sin(angle) * weight
    back = np.zeros((ROWS, 384))
    back[:LAGS, :LO] = c[:, :LO]
    back[:LAGS, LO:2 * LO] = -s[:, :LO]
    ch, sh = c[:, LO:], s[:, LO:]
    back[:LAGS, 256:256 + 4 * EXTRA] = np.concatenate([ch, ch, -sh, sh], axis=1)
    back[LAGS, 256 + EI] = 1.0
    back[LAGS + 1, 256 + EJ] = 1.0

    def split(t, axis):
        t = t.astype(np.float32)
        hi = t.astype(jnp.bfloat16)
        lo = (t - hi.astype(np.float32)).astype(jnp.bfloat16)
        return np.concatenate([hi, lo], axis=axis)

    return split(left, 1), split(right, 1), split(back, 0)


def spectrum(x, table, energy_lane, one_lane):
    d = jnp.dot(x, table, preferred_element_type=jnp.float32)
    d = d[:, :384] + d[:, 384:]
    xf = x.astype(jnp.float32)
    energy = jnp.sum(xf * xf, axis=1, keepdims=True)
    lane = lax.broadcasted_iota(jnp.int32, (1, 128), 1)
    third = jnp.where(lane == energy_lane, energy, d[:, 256:])
    third = jnp.where(lane == one_lane, 1.0, third)
    return d[:, :128], d[:, 128:256], third


def place():
    me = lax.axis_index("clu")
    return me >> 2, me & 3, (me >> 1) & 1, me & 1


def pack_kernel(cube_ref, rows_ref, local_ref, remote_ref, *refs):
    parts, own_ref, core_ref, chip_ref, sems = refs[:4], *refs[4:]
    row, step, _, _ = place()
    quarter = parts[0].shape[0]
    copies = [
        pltpu.make_async_copy(rows_ref.at[pl.ds(pl.multiple_of(((row + d) & 3) * quarter, quarter), quarter)], out, sems.at[d])
        for d, out in enumerate(parts)
    ]
    channels, _, width = cube_ref.shape
    size = cube_ref.shape[1] // 4
    outs = (own_ref, core_ref, chip_ref.at[0], chip_ref.at[1])
    for d, out in enumerate(outs):
        at = pl.multiple_of((step ^ d) * size, size)
        for c in range(channels):
            copies.append(pltpu.make_async_copy(
                cube_ref.at[c, pl.ds(at, size)], out.at[pl.ds(c * size, size)], sems.at[4 + d * channels + c]
            ))
    for copy in copies:
        copy.start()
    line = lax.broadcasted_iota(jnp.int32, (16, width), 0)
    for d, out in enumerate(outs):
        lists = jnp.zeros((16, width), jnp.float32)
        for n, ref in enumerate((local_ref, remote_ref)):
            listed = ref[pl.ds(step ^ d, 1), :].astype(jnp.float32)
            per = listed.shape[1] // width
            for k in range(per):
                lists = jnp.where(line == n * per + k, listed[:, k * width:(k + 1) * width], lists)
        out[pl.ds(channels * size, 16), :] = lists.astype(jnp.bfloat16)
    for copy in copies:
        copy.wait()


def pick_kernel(owners_ref, g0, g1, g2, g3, give_ref):
    row, step, _, _ = place()
    for d in (1, 3):
        behind = (row + 4 - (owners_ref[step ^ d] >> 2)) & 3
        for n, ref in enumerate((g0, g1, g2, g3)):

            @pl.when(behind == n)
            def _():
                give_ref[d // 2] = ref[...]


def core_kernel(owners_ref, g0, g1, g2, g3, got_ref, _, mine_ref, theirs_ref):
    row, step, _, core = place()
    for d, to in ((0, mine_ref), (2, theirs_ref)):
        owner = owners_ref[step ^ d]
        here = (owner & 1) == core
        behind = jnp.where(here, (row + 4 - (owner >> 2)) & 3, 4)
        for n, ref in enumerate((g0, g1, g2, g3)):

            @pl.when(behind == n)
            def _():
                to[...] = ref[...]

        @pl.when(behind == 4)
        def _():
            to[...] = got_ref[d // 2]


def chip_kernel(owners_ref, mine_ref, got_ref, out_ref):
    _, step, x, _ = place()
    here = ((owners_ref[step] >> 1) & 1) == x

    @pl.when(here)
    def _():
        out_ref[...] = mine_ref[...]

    @pl.when(jnp.logical_not(here))
    def _():
        out_ref[...] = got_ref[...]


def clear_rest(out_ref, channels):
    events = out_ref.shape[0] // 24
    for k in range(3):
        for c in range(channels, 8):
            out_ref[pl.ds(k * 8 + c, events, stride=24), :] = jnp.zeros((events, 128), jnp.float32)


def left_kernel(table_ref, b0, b1, b2, b3, out_ref):
    events = out_ref.shape[0] // 24 // 4
    channels = b0.shape[0] // events
    clear_rest(out_ref, channels)
    for q, w_ref in enumerate((b0, b1, b2, b3)):
        parts = spectrum(w_ref[:channels * events], table_ref[...], EI, EJ)
        for c in range(channels):
            for n, part in enumerate(parts):
                to = pl.ds(q * events * 24 + n * 8 + c, events, stride=24)
                out_ref[to, :] = part[c * events:(c + 1) * events]


def right_kernel(table_ref, p0, p1, p2, p3, out_ref):
    events = out_ref.shape[0] // 24
    clear_rest(out_ref, 4 * p0.shape[0] // events)
    row = place()[0]
    for behind, p_ref in ((0, p0), (1, p1), (3, p2), (2, p3)):
        base = ((row + 4 - behind) & 3) * p_ref.shape[0]
        x = p_ref[...]
        parts = spectrum(x, table_ref[...], EJ, EI)
        for g in range(x.shape[0] // 32):
            at = base + 32 * g
            c = at // events
            to = (at - c * events) * 24 + c
            for k, part in enumerate(parts):
                out_ref[pl.ds(to + 8 * k, 32, stride=24), :] = part[32 * g:32 * g + 32]


def channel_sum(vs, sub):
    for shift in (4, 2, 1):
        keep = (sub & shift) == 0
        half = len(vs) // 2
        vs = [
            jnp.where(keep, a + pltpu.roll(a, 8 - shift, 0), b + pltpu.roll(b, shift, 0))
            for a, b in zip(vs[:half], vs[half:])
        ]
    return vs[0]


MOVES = (2, 1, 3, 0)


def target(k, dz, dh, count):
    return ((k // 2 + dz) % (count // 2)) * 2 + (k % 2 + dh) % 2


def pair_kernel(across, token_ref, local_ref, remote_ref, left, right, back_ref, out_ref, next_ref, z):
    width = out_ref.shape[2]
    half = out_ref.shape[0]
    next_ref[0] = token_ref[0]
    sta = lax.axis_index("sta")
    share = width // 4
    pairs = local_ref.shape[0] // 4
    bh, bl = back_ref[:ROWS], back_ref[ROWS:]
    contract = (((1,), (1,)), ((), ()))
    dot = lambda a, b: lax.dot_general(a, b, contract, preferred_element_type=jnp.float32)
    sub = lax.broadcasted_iota(jnp.int32, (8, 128), 0)
    for t in range(half):
        first = target(sta, MOVES[t], across, 2 * half) * share

        def body(it, carry):
            for part in range(4):
                g = it * 4 + part
                q = g >> 3
                at = q * pairs + first + (g & 7) * 8
                products = [[], [], []]
                for p in range(8):
                    i = pl.multiple_of(local_ref[at + p], 8)
                    j = pl.multiple_of(remote_ref[at + p], 8)
                    xa, xb, xc = left[pl.ds(i, 8)], left[pl.ds(i + 8, 8)], left[pl.ds(i + 16, 8)]
                    ya, yb, yc = right[pl.ds(j, 8)], right[pl.ds(j + 8, 8)], right[pl.ds(j + 16, 8)]
                    for col, v in enumerate((xa * ya + xb * yb, xb * ya - xa * yb, xc * yc)):
                        products[col].append(v)
                to = pl.multiple_of(g * 8, 8)
                for col in range(3):
                    z[pl.ds(to, 8), col * 128:col * 128 + 128] = channel_sum(products[col], sub)
            return carry

        lax.fori_loop(0, width // 32, body, 0)
        zk = z[...]
        zh = zk.astype(jnp.bfloat16)
        zl = (zk - zh.astype(jnp.float32)).astype(jnp.bfloat16)
        out_ref[t] = dot(bh, zh) + dot(bh, zl) + dot(bl, zh)


def add_kernel(a_ref, b_ref, *out_refs):
    for t, ref in enumerate(out_refs):
        ref[...] = a_ref[t] + b_ref[t]


def sum_kernel(*refs):
    parts, out_refs = refs[:-4], refs[-4:]
    total = parts[0][...]
    for ref in parts[1:]:
        total = total + ref[...]
    count = CH * SAMP
    ni = 1.0 / jnp.sqrt(total[LAGS:LAGS + 1] / count + 1e-6)
    nj = 1.0 / jnp.sqrt(total[LAGS + 1:LAGS + 2] / count + 1e-6)
    total = total * (ni * nj / count)
    share = out_refs[0].shape[1]
    for q, ref in enumerate(out_refs):
        ref[...] = total[:, q * share:(q + 1) * share]


def final_kernel(near_ref, *refs):
    out_ref = refs[-1]
    step = place()[1]
    for r, ref in enumerate(refs[:-1]):
        s = step ^ r
        out_ref[0, s] = (ref[...] * near_ref[0, s].astype(jnp.float32)).T[:, :LAGS]


SMEM = pl.BlockSpec(memory_space=pltpu.SMEM)
VMEM = pl.BlockSpec(memory_space=pltpu.VMEM)
PARAMS = pltpu.CompilerParams(vmem_limit_bytes=20 * 1024 * 1024)
SMALL = pltpu.CompilerParams(vmem_limit_bytes=8 * 1024 * 1024)


def local(waves, owners, neighbours, pair_local, pair_remote):
    ev, ch, samp = waves.shape
    steps = owners.shape[0]
    pairs = pair_local.shape[2]
    n_clu, n_sta = lax.axis_size("clu"), lax.axis_size("sta")
    share = pairs // n_sta
    block = ev // steps
    left_table, right_table, back_table = (jnp.asarray(t) for t in tables())
    cube = waves.transpose(1, 0, 2)
    rows = cube.reshape(ch * ev, samp)
    f32, bf16 = jnp.float32, jnp.bfloat16
    shaped = jax.ShapeDtypeStruct

    me = lax.axis_index("clu")
    row, step = me // 4, me % 4
    near = lambda v, d: v if d == 0 else lax.ppermute(v, "clu", [(i, i ^ d) for i in range(n_clu)])
    turn = lambda v, d: lax.ppermute(v, "clu", [(i, (i + 4 * d) % n_clu) for i in range(n_clu)])

    quarter = ch * ev // 4
    piece = shaped((quarter, samp), bf16)
    height = ch * block + 16
    payload = shaped((height, samp), bf16)
    *parts, own, core, chip = pl.pallas_call(
        pack_kernel, out_shape=(piece,) * 4 + (payload, payload, shaped((2, height, samp), bf16)),
        in_specs=[pl.BlockSpec(memory_space=pl.ANY)] * 2 + [VMEM] * 2, out_specs=(VMEM,) * 7,
        scratch_shapes=[pltpu.SemaphoreType.DMA((4 + 4 * ch,))], compiler_params=SMALL, name="pack",
    )(cube, rows, pair_local[0], pair_remote[0])
    chip = near(chip, 2)
    blocks = [own, near(core, 1), chip[0], near(chip[1], 1)]
    got = [part if d == 0 else turn(part, d) for d, part in enumerate(parts)]
    give = pl.pallas_call(
        pick_kernel, out_shape=shaped((2, quarter, samp), bf16), in_specs=[SMEM] + [VMEM] * 4, out_specs=VMEM,
        compiler_params=SMALL, name="pick",
    )(owners, *got)
    mine, theirs = pl.pallas_call(
        core_kernel, out_shape=(piece, piece),
        in_specs=[SMEM] + [VMEM] * 5 + [pl.BlockSpec(memory_space=pl.ANY)], out_specs=(VMEM,) * 2,
        compiler_params=SMALL, name="over_core",
    )(owners, *got, near(give, 1), chip)
    mine = pl.pallas_call(
        chip_kernel, out_shape=piece, in_specs=[SMEM] + [VMEM] * 2, out_specs=VMEM,
        compiler_params=SMALL, name="over_x",
    )(owners, mine, near(theirs, 2))
    pieces = [mine] + [turn(mine, d) for d in (1, -1, 2)]

    listed = jnp.stack([b[ch * block:ch * block + 2 * pairs // samp] for b in blocks]).astype(jnp.int32)
    listed = listed.reshape(4, 2, pairs) * 24
    first = listed[:, 0] + jnp.arange(4, dtype=jnp.int32)[:, None] * (block * 24)
    first, second = first.reshape(4 * pairs), listed[:, 1].reshape(4 * pairs)

    spectra = shaped((ev * 24, 128), f32)
    cost = pl.CostEstimate(flops=2 * ch * ev * samp * 768, bytes_accessed=4000000, transcendentals=0)
    left = pl.pallas_call(
        left_kernel, out_shape=spectra, in_specs=[VMEM] * 5, out_specs=VMEM,
        compiler_params=PARAMS, name="left", cost_estimate=cost,
    )(left_table, *blocks)
    right = pl.pallas_call(
        right_kernel, out_shape=spectra, in_specs=[VMEM] * 5, out_specs=VMEM,
        compiler_params=PARAMS, name="right", cost_estimate=cost,
    )(right_table, *pieces)

    halves = []
    token = owners
    for across in (1, 0):
        raw, token = pl.pallas_call(
            functools.partial(pair_kernel, across),
            out_shape=(shaped((n_sta // 2, ROWS, 4 * share), f32), shaped((steps,), jnp.int32)),
            in_specs=[SMEM] * 3 + [VMEM] * 3, out_specs=(VMEM, SMEM),
            scratch_shapes=[pltpu.VMEM((4 * share, 384), f32)],
            compiler_params=PARAMS, name="pairs", cost_estimate=cost,
        )(token, first, second, left, right, back_table)
        halves.append(raw)
    hop = lambda v, dz, dh: lax.ppermute(v, "sta", [(k, target(k, dz, dh, n_sta)) for k in range(n_sta)])
    sums = pl.pallas_call(
        add_kernel, out_shape=(shaped((ROWS, 4 * share), f32),) * 4,
        in_specs=[VMEM] * 2, out_specs=(VMEM,) * 4, compiler_params=SMALL, name="add",
    )(hop(halves[0], 0, 1), halves[1])
    received = [v if dz == 0 else hop(v, dz, 0) for dz, v in zip(MOVES, sums)]

    done = pl.pallas_call(
        sum_kernel, out_shape=(shaped((ROWS, share), f32),) * 4,
        in_specs=[VMEM] * len(received), out_specs=(VMEM,) * 4, compiler_params=SMALL, name="total",
    )(*received)
    done = [near(v, d) for d, v in enumerate(done)]
    out = pl.pallas_call(
        final_kernel, out_shape=shaped((1, steps, share, LAGS), f32),
        in_specs=[SMEM] + [VMEM] * 4, out_specs=VMEM, compiler_params=SMALL, name="finish",
    )(neighbours, *done)
    return out.transpose(0, 1, 3, 2)


def solution(mesh):
    placed = (
        P("clu", "sta", None),
        P(),
        P("clu", None),
        P("clu", None, None),
        P("clu", None, None),
    )
    return jax.shard_map(
        local, mesh=mesh, in_specs=placed, out_specs=P("clu", None, None, "sta"), check_vma=False
    )
```

```python
import functools
import math

import jax
import jax.numpy as jnp
import numpy as np
from jax import lax
from jax.experimental import pallas as pl
from jax.experimental.pallas import tpu as pltpu
from jax.sharding import PartitionSpec as P

CH, SAMP, HALF, LAGS = 48, 256, 32, 65
CLU, STA = ("y", "xl", "core"), ("z", "xh")
N = 288
LO, EXTRA = 128, 17
ROWS = 72
TALL = 40
EI, EJ = 68, 69


def tables():
    u = np.arange(SAMP)[:, None]
    k = np.arange(N // 2 + 1)[None, :]
    angle = 2 * math.pi * ((u * k) % N) / N
    c, s = np.cos(angle), np.sin(angle)
    ch, sh = c[:, LO:], s[:, LO:]
    pad = np.zeros((SAMP, 128 - 4 * EXTRA))
    left = np.concatenate([c[:, :LO], s[:, :LO], ch, sh, sh, ch, pad], axis=1)
    right = np.concatenate([c[:, :LO], s[:, :LO], ch, sh, ch, sh, pad], axis=1)
    lag = np.arange(LAGS)[:, None] - HALF
    angle = 2 * math.pi * ((lag * k) % N) / N
    weight = np.where((k == 0) | (k == N // 2), 1.0, 2.0) / N
    c, s = np.cos(angle) * weight, np.sin(angle) * weight
    back = np.zeros((ROWS, 384))
    back[:LAGS, :LO] = c[:, :LO]
    back[:LAGS, LO:2 * LO] = -s[:, :LO]
    ch, sh = c[:, LO:], s[:, LO:]
    back[:LAGS, 256:256 + 4 * EXTRA] = np.concatenate([ch, ch, -sh, sh], axis=1)
    back[LAGS, 256 + EI] = 1.0
    back[LAGS + 1, 256 + EJ] = 1.0

    def split(t, axis):
        t = t.astype(np.float32)
        hi = t.astype(jnp.bfloat16)
        lo = (t - hi.astype(np.float32)).astype(jnp.bfloat16)
        return np.concatenate([hi, lo], axis=axis)

    return split(left, 1), split(right, 1), split(back, 0)


def spectrum(x, table, energy_lane, one_lane):
    d = jnp.dot(x, table, preferred_element_type=jnp.float32)
    d = d[:, :384] + d[:, 384:]
    xf = x.astype(jnp.float32)
    energy = jnp.sum(xf * xf, axis=1, keepdims=True)
    lane = lax.broadcasted_iota(jnp.int32, (1, 128), 1)
    third = jnp.where(lane == energy_lane, energy, d[:, 256:])
    third = jnp.where(lane == one_lane, 1.0, third)
    return d[:, :128], d[:, 128:256], third


def place():
    x, core = lax.axis_index("xl"), lax.axis_index("core")
    return lax.axis_index("y"), x * 2 + core, x, core


def cut_kernel(rows_ref, *refs):
    outs, sems = refs[:-1], refs[-1]
    row = place()[0]
    size = outs[0].shape[0]
    copies = [
        pltpu.make_async_copy(rows_ref.at[pl.ds(pl.multiple_of(((row + d) & 3) * size, size), size)], out, sems.at[d])
        for d, out in enumerate(outs)
    ]
    for copy in copies:
        copy.start()
    for copy in copies:
        copy.wait()


def pack_kernel(_, cube_ref, local_ref, remote_ref, own_ref, core_ref, chip_ref, lists_ref, sems):
    step = place()[1]
    channels, _, width = cube_ref.shape
    size = cube_ref.shape[1] // 4
    outs = (own_ref, core_ref, chip_ref.at[0], chip_ref.at[1])
    first = [pltpu.make_async_copy(ref.at[0], lists_ref.at[n], sems.at[n]) for n, ref in enumerate((local_ref, remote_ref))]
    copies = []
    for d, out in enumerate(outs):
        at = pl.multiple_of((step ^ d) * size, size)
        for c in range(channels):
            copies.append(pltpu.make_async_copy(
                cube_ref.at[c, pl.ds(at, size)], out.at[pl.ds(c * size, size)], sems.at[2 + d * channels + c]
            ))
    for copy in first + copies:
        copy.start()
    for copy in first:
        copy.wait()
    line = lax.broadcasted_iota(jnp.int32, (16, width), 0)
    for d, out in enumerate(outs):
        lists = jnp.zeros((16, width), jnp.float32)
        for n in range(2):
            listed = lists_ref[n, pl.ds(step ^ d, 1), :].astype(jnp.float32)
            per = listed.shape[1] // width
            for k in range(per):
                lists = jnp.where(line == n * per + k, listed[:, k * width:(k + 1) * width], lists)
        out[pl.ds(channels * size, 16), :] = lists.astype(jnp.bfloat16)
    for copy in copies:
        copy.wait()


def pick_kernel(owners_ref, g0, g1, g2, g3, _, give_ref):
    row, step, _, _ = place()
    for d in (1, 3):
        behind = (row + 4 - (owners_ref[step ^ d] >> 2)) & 3
        for n, ref in enumerate((g0, g1, g2, g3)):

            @pl.when(behind == n)
            def _():
                give_ref[d // 2] = ref[...]


def core_kernel(owners_ref, g0, g1, g2, g3, got_ref, _, mine_ref, theirs_ref):
    row, step, _, core = place()
    for d, to in ((0, mine_ref), (2, theirs_ref)):
        owner = owners_ref[step ^ d]
        here = (owner & 1) == core
        behind = jnp.where(here, (row + 4 - (owner >> 2)) & 3, 4)
        for n, ref in enumerate((g0, g1, g2, g3)):

            @pl.when(behind == n)
            def _():
                to[...] = ref[...]

        @pl.when(behind == 4)
        def _():
            to[...] = got_ref[d // 2]


def chip_kernel(owners_ref, mine_ref, got_ref, out_ref):
    _, step, x, _ = place()
    here = ((owners_ref[step] >> 1) & 1) == x

    @pl.when(here)
    def _():
        out_ref[...] = mine_ref[...]

    @pl.when(jnp.logical_not(here))
    def _():
        out_ref[...] = got_ref[...]


def clear_rest(out_ref, channels):
    events = out_ref.shape[0] // 24
    for k in range(3):
        for c in range(channels, 8):
            out_ref[pl.ds(k * 8 + c, events, stride=24), :] = jnp.zeros((events, 128), jnp.float32)


def left_kernel(table_ref, b0, b1, b2, b3, out_ref):
    events = out_ref.shape[0] // 24 // 4
    channels = b0.shape[0] // events
    clear_rest(out_ref, channels)
    for q, w_ref in enumerate((b0, b1, b2, b3)):
        parts = spectrum(w_ref[:channels * events], table_ref[...], EI, EJ)
        for c in range(channels):
            for n, part in enumerate(parts):
                to = pl.ds(q * events * 24 + n * 8 + c, events, stride=24)
                out_ref[to, :] = part[c * events:(c + 1) * events]


def right_kernel(table_ref, p0, p1, p2, p3, out_ref):
    events = out_ref.shape[0] // 24
    clear_rest(out_ref, 4 * p0.shape[0] // events)
    row = place()[0]
    for behind, p_ref in ((0, p0), (1, p1), (3, p2), (2, p3)):
        base = ((row + 4 - behind) & 3) * p_ref.shape[0]
        x = p_ref[...]
        parts = spectrum(x, table_ref[...], EJ, EI)
        for g in range(x.shape[0] // 32):
            at = base + 32 * g
            c = at // events
            to = (at - c * events) * 24 + c
            for k, part in enumerate(parts):
                out_ref[pl.ds(to + 8 * k, 32, stride=24), :] = part[32 * g:32 * g + 32]


def channel_sum(vs, sub):
    for shift in (4, 2, 1):
        keep = (sub & shift) == 0
        half = len(vs) // 2
        vs = [
            jnp.where(keep, a + pltpu.roll(a, 8 - shift, 0), b + pltpu.roll(b, shift, 0))
            for a, b in zip(vs[:half], vs[half:])
        ]
    return vs[0]


MOVES = (2, 1, 3, 0)


def target(k, dz, dh, count):
    return ((k // 2 + dz) % (count // 2)) * 2 + (k % 2 + dh) % 2


def pair_kernel(across, token_ref, local_ref, remote_ref, left, right, back_ref, out_ref, next_ref, z):
    width = out_ref.shape[2]
    half = out_ref.shape[0]
    next_ref[0] = token_ref[0]
    sta = lax.axis_index(STA)
    share = width // 4
    pairs = local_ref.shape[0] // 4
    bh, bl = back_ref[:ROWS], back_ref[ROWS:]
    contract = (((1,), (1,)), ((), ()))
    dot = lambda a, b: lax.dot_general(a, b, contract, preferred_element_type=jnp.float32)
    sub = lax.broadcasted_iota(jnp.int32, (8, 128), 0)
    for t in range(half):
        first = target(sta, MOVES[t], across, 2 * half) * share

        def body(it, carry):
            for part in range(4):
                g = it * 4 + part
                q = g >> 3
                at = q * pairs + first + (g & 7) * 8
                products = [[], [], []]
                for p in range(8):
                    i = pl.multiple_of(local_ref[at + p], 8)
                    j = pl.multiple_of(remote_ref[at + p], 8)
                    xa, xb, xc = left[pl.ds(i, 8)], left[pl.ds(i + 8, 8)], left[pl.ds(i + 16, 8)]
                    ya, yb, yc = right[pl.ds(j, 8)], right[pl.ds(j + 8, 8)], right[pl.ds(j + 16, 8)]
                    for col, v in enumerate((xa * ya + xb * yb, xb * ya - xa * yb, xc * yc)):
                        products[col].append(v)
                to = pl.multiple_of(g * 8, 8)
                for col in range(3):
                    z[pl.ds(to, 8), col * 128:col * 128 + 128] = channel_sum(products[col], sub)
            return carry

        lax.fori_loop(0, width // 32, body, 0)
        zk = z[...]
        zh = zk.astype(jnp.bfloat16)
        zl = (zk - zh.astype(jnp.float32)).astype(jnp.bfloat16)
        out_ref[t] = dot(bh, zh) + dot(bh, zl) + dot(bl, zh)


def add_kernel(a_ref, b_ref, out_ref):
    z, step = lax.axis_index("z"), place()[1]
    share = a_ref.shape[2] // 4
    for t, dz in enumerate(MOVES):
        total = a_ref[t] + b_ref[t]
        for q in range(4):
            part = total[:, q * share:(q + 1) * share]
            slot = ((z + dz) & 3) * 4 + (step ^ q)
            out_ref[slot, :, :share] = part[:TALL]
            out_ref[slot, :ROWS - TALL, share:] = part[TALL:]


def final_kernel(near_ref, got_ref, out_ref):
    share = out_ref.shape[2]
    count = CH * SAMP
    for s in range(4):
        total = (got_ref[s] + got_ref[4 + s]) + (got_ref[8 + s] + got_ref[12 + s])
        total = jnp.concatenate([total[:, :share], total[:ROWS - TALL, share:]], axis=0)
        ni = 1.0 / jnp.sqrt(total[LAGS:LAGS + 1] / count + 1e-6)
        nj = 1.0 / jnp.sqrt(total[LAGS + 1:LAGS + 2] / count + 1e-6)
        out_ref[0, s] = (total * (ni * nj / count * near_ref[0, s].astype(jnp.float32))).T[:, :LAGS]


HBM = pl.BlockSpec(memory_space=pltpu.HBM)
ANY = pl.BlockSpec(memory_space=pl.ANY)
SMEM = pl.BlockSpec(memory_space=pltpu.SMEM)
VMEM = pl.BlockSpec(memory_space=pltpu.VMEM)
PARAMS = pltpu.CompilerParams(vmem_limit_bytes=20 * 1024 * 1024)
SMALL = pltpu.CompilerParams(vmem_limit_bytes=8 * 1024 * 1024)


def in_hbm(v):
    return pltpu.with_memory_space_constraint(v, pltpu.HBM)


def local(waves, owners, neighbours, pair_local, pair_remote):
    ev, ch, samp = waves.shape
    steps = owners.shape[0]
    pairs = pair_local.shape[2]
    n_clu, n_sta = lax.axis_size(CLU), lax.axis_size(STA)
    share = pairs // n_sta
    block = ev // steps
    left_table, right_table, back_table = (jnp.asarray(t) for t in tables())
    cube = waves.transpose(1, 0, 2)
    rows = cube.reshape(ch * ev, samp)
    f32, bf16 = jnp.float32, jnp.bfloat16
    shaped = jax.ShapeDtypeStruct

    me = lax.axis_index(CLU)
    row, step = me // 4, me % 4
    near = lambda v, d: v if d == 0 else lax.ppermute(v, CLU, [(i, i ^ d) for i in range(n_clu)])
    turn = lambda v, d: lax.ppermute(v, CLU, [(i, (i + 4 * d) % n_clu) for i in range(n_clu)])

    quarter = ch * ev // 4
    piece = shaped((quarter, samp), bf16)
    height = ch * block + 16
    payload = shaped((height, samp), bf16)
    parts = pl.pallas_call(
        cut_kernel, out_shape=(piece,) * 4, in_specs=[HBM], out_specs=(VMEM,) * 4,
        scratch_shapes=[pltpu.SemaphoreType.DMA((4,))], compiler_params=SMALL, name="cut",
    )(in_hbm(rows))
    own, core, chip = pl.pallas_call(
        pack_kernel, out_shape=(payload, payload, shaped((2, height, samp), bf16)),
        in_specs=[ANY] + [HBM] * 3, out_specs=(VMEM,) * 3,
        scratch_shapes=[pltpu.VMEM((2, steps, pairs), jnp.int32), pltpu.SemaphoreType.DMA((2 + 4 * ch,))],
        compiler_params=SMALL, name="pack",
    )(parts[0], in_hbm(cube), in_hbm(pair_local), in_hbm(pair_remote))
    chip = near(chip, 2)
    blocks = [own, near(core, 1), chip[0], near(chip[1], 1)]
    got = [part if d == 0 else turn(part, d) for d, part in enumerate(parts)]
    give = pl.pallas_call(
        pick_kernel, out_shape=shaped((2, quarter, samp), bf16), in_specs=[SMEM] + [VMEM] * 4 + [ANY], out_specs=VMEM,
        compiler_params=SMALL, name="pick",
    )(in_hbm(owners), *got, own)
    mine, theirs = pl.pallas_call(
        core_kernel, out_shape=(piece, piece),
        in_specs=[SMEM] + [VMEM] * 5 + [ANY], out_specs=(VMEM,) * 2,
        compiler_params=SMALL, name="over_core",
    )(in_hbm(owners), *got, near(give, 1), chip)
    mine = pl.pallas_call(
        chip_kernel, out_shape=piece, in_specs=[SMEM] + [VMEM] * 2, out_specs=VMEM,
        compiler_params=SMALL, name="over_x",
    )(in_hbm(owners), mine, near(theirs, 2))
    pieces = [mine] + [turn(mine, d) for d in (1, -1, 2)]

    listed = jnp.stack([b[ch * block:ch * block + 2 * pairs // samp] for b in blocks]).astype(jnp.int32)
    listed = listed.reshape(4, 2, pairs) * 24
    first = listed[:, 0] + jnp.arange(4, dtype=jnp.int32)[:, None] * (block * 24)
    first, second = first.reshape(4 * pairs), listed[:, 1].reshape(4 * pairs)

    spectra = shaped((ev * 24, 128), f32)
    cost = pl.CostEstimate(flops=2 * ch * ev * samp * 768, bytes_accessed=4000000, transcendentals=0)
    left = pl.pallas_call(
        left_kernel, out_shape=spectra, in_specs=[VMEM] * 5, out_specs=VMEM,
        compiler_params=PARAMS, name="left", cost_estimate=cost,
    )(left_table, *blocks)
    right = pl.pallas_call(
        right_kernel, out_shape=spectra, in_specs=[VMEM] * 5, out_specs=VMEM,
        compiler_params=PARAMS, name="right", cost_estimate=cost,
    )(right_table, *pieces)

    halves = []
    token = owners
    for across in (1, 0):
        raw, token = pl.pallas_call(
            functools.partial(pair_kernel, across),
            out_shape=(shaped((n_sta // 2, ROWS, 4 * share), f32), shaped((steps,), jnp.int32)),
            in_specs=[SMEM] * 3 + [VMEM] * 3, out_specs=(VMEM, SMEM),
            scratch_shapes=[pltpu.VMEM((4 * share, 384), f32)],
            compiler_params=PARAMS, name="pairs", cost_estimate=cost,
        )(token, first, second, left, right, back_table)
        halves.append(raw)
    hop = lambda v, dz, dh: lax.ppermute(v, STA, [(k, target(k, dz, dh, n_sta)) for k in range(n_sta)])
    slots = pl.pallas_call(
        add_kernel, out_shape=shaped((2 * n_sta, TALL, 2 * share), f32), in_specs=[VMEM] * 2, out_specs=VMEM,
        compiler_params=SMALL, name="add",
    )(hop(halves[0], 0, 1), halves[1])
    slots = lax.all_to_all(slots, ("z", "xl", "core"), 0, 0)
    out = pl.pallas_call(
        final_kernel, out_shape=shaped((1, steps, share, LAGS), f32),
        in_specs=[SMEM, VMEM], out_specs=VMEM, compiler_params=SMALL, name="finish",
    )(in_hbm(neighbours), slots)
    return out.transpose(0, 1, 3, 2)


def solution(mesh):
    fine = jax.sharding.Mesh(mesh.devices.reshape(4, 2, 2, 4, 2), CLU + STA)
    placed = (
        P(CLU, STA, None),
        P(),
        P(CLU, None),
        P(CLU, None, None),
        P(CLU, None, None),
    )
    return jax.shard_map(
        local, mesh=fine, in_specs=placed, out_specs=P(CLU, None, None, STA), check_vma=False
    )
```

```python
import functools
import math

import jax
import jax.numpy as jnp
import numpy as np
from jax import lax
from jax.experimental import pallas as pl
from jax.experimental.pallas import tpu as pltpu
from jax.sharding import PartitionSpec as P

CH, SAMP, HALF, LAGS = 48, 256, 32, 65
CLU, STA = ("y", "xl", "core"), ("z", "xh")
N = 288
LO, EXTRA = 128, 17
ROWS = 72
TALL = 40
EI, EJ = 68, 69


def tables():
    u = np.arange(SAMP)[:, None]
    k = np.arange(N // 2 + 1)[None, :]
    angle = 2 * math.pi * ((u * k) % N) / N
    c, s = np.cos(angle), np.sin(angle)
    ch, sh = c[:, LO:], s[:, LO:]
    pad = np.zeros((SAMP, 128 - 4 * EXTRA))
    left = np.concatenate([c[:, :LO], s[:, :LO], ch, sh, sh, ch, pad], axis=1)
    right = np.concatenate([c[:, :LO], s[:, :LO], ch, sh, ch, sh, pad], axis=1)
    lag = np.arange(LAGS)[:, None] - HALF
    angle = 2 * math.pi * ((lag * k) % N) / N
    weight = np.where((k == 0) | (k == N // 2), 1.0, 2.0) / N
    c, s = np.cos(angle) * weight, np.sin(angle) * weight
    back = np.zeros((ROWS, 384))
    back[:LAGS, :LO] = c[:, :LO]
    back[:LAGS, LO:2 * LO] = -s[:, :LO]
    ch, sh = c[:, LO:], s[:, LO:]
    back[:LAGS, 256:256 + 4 * EXTRA] = np.concatenate([ch, ch, -sh, sh], axis=1)
    back[LAGS, 256 + EI] = 1.0
    back[LAGS + 1, 256 + EJ] = 1.0

    def split(t, axis):
        t = t.astype(np.float32)
        hi = t.astype(jnp.bfloat16)
        lo = (t - hi.astype(np.float32)).astype(jnp.bfloat16)
        return np.concatenate([hi, lo], axis=axis)

    return split(left, 1), split(right, 1), split(back, 0)


def spectrum(x, table, energy_lane, one_lane):
    d = jnp.dot(x, table, preferred_element_type=jnp.float32)
    d = d[:, :384] + d[:, 384:]
    xf = x.astype(jnp.float32)
    energy = jnp.sum(xf * xf, axis=1, keepdims=True)
    lane = lax.broadcasted_iota(jnp.int32, (1, 128), 1)
    third = jnp.where(lane == energy_lane, energy, d[:, 256:])
    third = jnp.where(lane == one_lane, 1.0, third)
    return d[:, :128], d[:, 128:256], third


def place():
    x, core = lax.axis_index("xl"), lax.axis_index("core")
    return lax.axis_index("y"), x * 2 + core, x, core


def pack_kernel(rows_ref, cube_ref, local_ref, remote_ref, *refs):
    parts, (own_ref, core_ref, chip_ref, lists_ref, sems) = refs[:4], refs[4:]
    row, step, _, _ = place()
    quarter = parts[0].shape[0]
    cuts = [
        pltpu.make_async_copy(rows_ref.at[pl.ds(pl.multiple_of(((row + d) & 3) * quarter, quarter), quarter)], out, sems.at[d])
        for d, out in enumerate(parts)
    ]
    channels, _, width = cube_ref.shape
    size = cube_ref.shape[1] // 4
    outs = (own_ref, core_ref, chip_ref.at[0], chip_ref.at[1])
    first = [pltpu.make_async_copy(ref.at[0], lists_ref.at[n], sems.at[4 + n]) for n, ref in enumerate((local_ref, remote_ref))]
    copies = []
    for d, out in enumerate(outs):
        at = pl.multiple_of((step ^ d) * size, size)
        for c in range(channels):
            copies.append(pltpu.make_async_copy(
                cube_ref.at[c, pl.ds(at, size)], out.at[pl.ds(c * size, size)], sems.at[6 + d * channels + c]
            ))
    for copy in first + cuts + copies:
        copy.start()
    for copy in first:
        copy.wait()
    line = lax.broadcasted_iota(jnp.int32, (16, width), 0)
    for d, out in enumerate(outs):
        lists = jnp.zeros((16, width), jnp.float32)
        for n in range(2):
            listed = lists_ref[n, pl.ds(step ^ d, 1), :].astype(jnp.float32)
            per = listed.shape[1] // width
            for k in range(per):
                lists = jnp.where(line == n * per + k, listed[:, k * width:(k + 1) * width], lists)
        out[pl.ds(channels * size, 16), :] = lists.astype(jnp.bfloat16)
    for copy in cuts + copies:
        copy.wait()


def pick_kernel(owners_ref, g0, g1, g2, g3, give_ref):
    row, step, _, _ = place()
    for d in (1, 3):
        behind = (row + 4 - (owners_ref[step ^ d] >> 2)) & 3
        for n, ref in enumerate((g0, g1, g2, g3)):

            @pl.when(behind == n)
            def _():
                give_ref[d // 2] = ref[...]


def core_kernel(owners_ref, g0, g1, g2, g3, got_ref, _, mine_ref, theirs_ref):
    row, step, _, core = place()
    for d, to in ((0, mine_ref), (2, theirs_ref)):
        owner = owners_ref[step ^ d]
        here = (owner & 1) == core
        behind = jnp.where(here, (row + 4 - (owner >> 2)) & 3, 4)
        for n, ref in enumerate((g0, g1, g2, g3)):

            @pl.when(behind == n)
            def _():
                to[...] = ref[...]

        @pl.when(behind == 4)
        def _():
            to[...] = got_ref[d // 2]


def chip_kernel(owners_ref, mine_ref, got_ref, out_ref):
    _, step, x, _ = place()
    here = ((owners_ref[step] >> 1) & 1) == x

    @pl.when(here)
    def _():
        out_ref[...] = mine_ref[...]

    @pl.when(jnp.logical_not(here))
    def _():
        out_ref[...] = got_ref[...]


def clear_rest(out_ref, channels):
    events = out_ref.shape[0] // 24
    for k in range(3):
        for c in range(channels, 8):
            out_ref[pl.ds(k * 8 + c, events, stride=24), :] = jnp.zeros((events, 128), jnp.float32)


def left_kernel(table_ref, b0, b1, b2, b3, out_ref):
    events = out_ref.shape[0] // 24 // 4
    channels = b0.shape[0] // events
    clear_rest(out_ref, channels)
    for q, w_ref in enumerate((b0, b1, b2, b3)):
        parts = spectrum(w_ref[:channels * events], table_ref[...], EI, EJ)
        for c in range(channels):
            for n, part in enumerate(parts):
                to = pl.ds(q * events * 24 + n * 8 + c, events, stride=24)
                out_ref[to, :] = part[c * events:(c + 1) * events]


def right_kernel(table_ref, p0, p1, p2, p3, out_ref):
    events = out_ref.shape[0] // 24
    clear_rest(out_ref, 4 * p0.shape[0] // events)
    row = place()[0]
    for behind, p_ref in ((0, p0), (1, p1), (3, p2), (2, p3)):
        base = ((row + 4 - behind) & 3) * p_ref.shape[0]
        x = p_ref[...]
        parts = spectrum(x, table_ref[...], EJ, EI)
        for g in range(x.shape[0] // 32):
            at = base + 32 * g
            c = at // events
            to = (at - c * events) * 24 + c
            for k, part in enumerate(parts):
                out_ref[pl.ds(to + 8 * k, 32, stride=24), :] = part[32 * g:32 * g + 32]


def channel_sum(vs, sub):
    for shift in (4, 2, 1):
        keep = (sub & shift) == 0
        half = len(vs) // 2
        couples = list(zip(vs[:half], vs[half:]))
        if shift == 4:
            vs = [jnp.where(keep, a, b) + pltpu.roll(jnp.where(keep, b, a), 4, 0) for a, b in couples]
        else:
            vs = [jnp.where(keep, a + pltpu.roll(a, 8 - shift, 0), b + pltpu.roll(b, shift, 0)) for a, b in couples]
    return vs[0]


MOVES = (2, 1, 3, 0)


def target(k, dz, dh, count):
    return ((k // 2 + dz) % (count // 2)) * 2 + (k % 2 + dh) % 2


def pair_kernel(across, token_ref, local_ref, remote_ref, left, right, back_ref, out_ref, next_ref, z):
    width = out_ref.shape[2]
    half = out_ref.shape[0]
    next_ref[0] = token_ref[0]
    sta = lax.axis_index(STA)
    share = width // 4
    pairs = local_ref.shape[0] // 4
    back = back_ref[...]
    contract = (((1,), (1,)), ((), ()))
    dot = lambda a, b: lax.dot_general(a, b, contract, preferred_element_type=jnp.float32)
    sub = lax.broadcasted_iota(jnp.int32, (8, 128), 0)
    for t in range(half):
        first = target(sta, MOVES[t], across, 2 * half) * share

        def body(it, carry):
            sums = []
            for part in range(8):
                g = it * 8 + part
                q = g >> 3
                at = q * pairs + first + (g & 7) * 8
                products = [[], [], []]
                for p in range(8):
                    i = pl.multiple_of(local_ref[at + p], 8)
                    j = pl.multiple_of(remote_ref[at + p], 8)
                    xa, xb, xc = left[pl.ds(i, 8)], left[pl.ds(i + 8, 8)], left[pl.ds(i + 16, 8)]
                    ya, yb, yc = right[pl.ds(j, 8)], right[pl.ds(j + 8, 8)], right[pl.ds(j + 16, 8)]
                    for col, v in enumerate((xa * ya + xb * yb, xb * ya - xa * yb, xc * yc)):
                        products[col].append(v)
                sums += [(g, col, channel_sum(products[col], sub)) for col in range(3)]
            for g, col, v in sums:
                z[pl.ds(pl.multiple_of(g * 8, 8), 8), col * 128:col * 128 + 128] = v
            return carry

        lax.fori_loop(0, width // 64, body, 0)
        zk = z[...]
        zh = zk.astype(jnp.bfloat16)
        zl = (zk - zh.astype(jnp.float32)).astype(jnp.bfloat16)
        high = dot(back, zh)
        out_ref[t] = high[:ROWS] + high[ROWS:] + dot(back[:ROWS], zl)


def add_kernel(a_ref, b_ref, out_ref):
    z, step = lax.axis_index("z"), place()[1]
    share = a_ref.shape[2] // 4
    for t, dz in enumerate(MOVES):
        total = a_ref[t] + b_ref[t]
        for q in range(4):
            part = total[:, q * share:(q + 1) * share]
            slot = ((z + dz) & 3) * 4 + (step ^ q)
            out_ref[slot, :, :share] = part[:TALL]
            out_ref[slot, :ROWS - TALL, share:] = part[TALL:]


def final_kernel(near_ref, got_ref, out_ref):
    share = out_ref.shape[2]
    count = CH * SAMP
    for s in range(4):
        total = (got_ref[s] + got_ref[4 + s]) + (got_ref[8 + s] + got_ref[12 + s])
        total = jnp.concatenate([total[:, :share], total[:ROWS - TALL, share:]], axis=0)
        ni = 1.0 / jnp.sqrt(total[LAGS:LAGS + 1] / count + 1e-6)
        nj = 1.0 / jnp.sqrt(total[LAGS + 1:LAGS + 2] / count + 1e-6)
        out_ref[0, s] = (total * (ni * nj / count * near_ref[0, s].astype(jnp.float32))).T[:, :LAGS]


HBM = pl.BlockSpec(memory_space=pltpu.HBM)
ANY = pl.BlockSpec(memory_space=pl.ANY)
SMEM = pl.BlockSpec(memory_space=pltpu.SMEM)
VMEM = pl.BlockSpec(memory_space=pltpu.VMEM)
PARAMS = pltpu.CompilerParams(vmem_limit_bytes=20 * 1024 * 1024)
SMALL = pltpu.CompilerParams(vmem_limit_bytes=8 * 1024 * 1024)


def in_hbm(v):
    return pltpu.with_memory_space_constraint(v, pltpu.HBM)


def local(waves, owners, neighbours, pair_local, pair_remote):
    ev, ch, samp = waves.shape
    steps = owners.shape[0]
    pairs = pair_local.shape[2]
    n_clu, n_sta = lax.axis_size(CLU), lax.axis_size(STA)
    share = pairs // n_sta
    block = ev // steps
    left_table, right_table, back_table = (jnp.asarray(t) for t in tables())
    cube = waves.transpose(1, 0, 2)
    rows = cube.reshape(ch * ev, samp)
    f32, bf16 = jnp.float32, jnp.bfloat16
    shaped = jax.ShapeDtypeStruct

    me = lax.axis_index(CLU)
    row, step = me // 4, me % 4
    near = lambda v, d: v if d == 0 else lax.ppermute(v, CLU, [(i, i ^ d) for i in range(n_clu)])
    turn = lambda v, d: lax.ppermute(v, CLU, [(i, (i + 4 * d) % n_clu) for i in range(n_clu)])

    quarter = ch * ev // 4
    piece = shaped((quarter, samp), bf16)
    height = ch * block + 16
    payload = shaped((height, samp), bf16)
    *parts, own, core, chip = pl.pallas_call(
        pack_kernel, out_shape=(piece,) * 4 + (payload, payload, shaped((2, height, samp), bf16)),
        in_specs=[HBM] * 4, out_specs=(VMEM,) * 7,
        scratch_shapes=[pltpu.VMEM((2, steps, pairs), jnp.int32), pltpu.SemaphoreType.DMA((6 + 4 * ch,))],
        compiler_params=SMALL, name="pack",
    )(in_hbm(rows), in_hbm(cube), in_hbm(pair_local), in_hbm(pair_remote))
    chip = near(chip, 2)
    blocks = [own, near(core, 1), chip[0], near(chip[1], 1)]
    got = [part if d == 0 else turn(part, d) for d, part in enumerate(parts)]
    give = pl.pallas_call(
        pick_kernel, out_shape=shaped((2, quarter, samp), bf16), in_specs=[SMEM] + [VMEM] * 4, out_specs=VMEM,
        compiler_params=SMALL, name="pick",
    )(in_hbm(owners), *got)
    mine, theirs = pl.pallas_call(
        core_kernel, out_shape=(piece, piece),
        in_specs=[SMEM] + [VMEM] * 5 + [ANY], out_specs=(VMEM,) * 2,
        compiler_params=SMALL, name="over_core",
    )(in_hbm(owners), *got, near(give, 1), chip)
    mine = pl.pallas_call(
        chip_kernel, out_shape=piece, in_specs=[SMEM] + [VMEM] * 2, out_specs=VMEM,
        compiler_params=SMALL, name="over_x",
    )(in_hbm(owners), mine, near(theirs, 2))
    pieces = [mine] + [turn(mine, d) for d in (1, -1, 2)]

    listed = jnp.stack([b[ch * block:ch * block + 2 * pairs // samp] for b in blocks]).astype(jnp.int32)
    listed = listed.reshape(4, 2, pairs) * 24
    first = listed[:, 0] + jnp.arange(4, dtype=jnp.int32)[:, None] * (block * 24)
    first, second = first.reshape(4 * pairs), listed[:, 1].reshape(4 * pairs)

    spectra = shaped((ev * 24, 128), f32)
    cost = pl.CostEstimate(flops=2 * ch * ev * samp * 768, bytes_accessed=4000000, transcendentals=0)
    left = pl.pallas_call(
        left_kernel, out_shape=spectra, in_specs=[VMEM] * 5, out_specs=VMEM,
        compiler_params=PARAMS, name="left", cost_estimate=cost,
    )(left_table, *blocks)
    right = pl.pallas_call(
        right_kernel, out_shape=spectra, in_specs=[VMEM] * 5, out_specs=VMEM,
        compiler_params=PARAMS, name="right", cost_estimate=cost,
    )(right_table, *pieces)

    halves = []
    token = owners
    for across in (1, 0):
        raw, token = pl.pallas_call(
            functools.partial(pair_kernel, across),
            out_shape=(shaped((n_sta // 2, ROWS, 4 * share), f32), shaped((steps,), jnp.int32)),
            in_specs=[SMEM] * 3 + [VMEM] * 3, out_specs=(VMEM, SMEM),
            scratch_shapes=[pltpu.VMEM((4 * share, 384), f32)],
            compiler_params=PARAMS, name="pairs", cost_estimate=cost,
        )(token, first, second, left, right, back_table)
        halves.append(raw)
    hop = lambda v, dz, dh: lax.ppermute(v, STA, [(k, target(k, dz, dh, n_sta)) for k in range(n_sta)])
    slots = pl.pallas_call(
        add_kernel, out_shape=shaped((2 * n_sta, TALL, 2 * share), f32), in_specs=[VMEM] * 2, out_specs=VMEM,
        compiler_params=SMALL, name="add",
    )(hop(halves[0], 0, 1), halves[1])
    slots = lax.all_to_all(slots, ("z", "xl", "core"), 0, 0)
    out = pl.pallas_call(
        final_kernel, out_shape=shaped((1, steps, share, LAGS), f32),
        in_specs=[SMEM, VMEM], out_specs=VMEM, compiler_params=SMALL, name="finish",
    )(in_hbm(neighbours), slots)
    return out.transpose(0, 1, 3, 2)


def solution(mesh):
    fine = jax.sharding.Mesh(mesh.devices.reshape(4, 2, 2, 4, 2), CLU + STA)
    placed = (
        P(CLU, STA, None),
        P(),
        P(CLU, None),
        P(CLU, None, None),
        P(CLU, None, None),
    )
    return jax.shard_map(
        local, mesh=fine, in_specs=placed, out_specs=P(CLU, None, None, STA), check_vma=False
    )
```

```python
import functools
import math

import jax
import jax.numpy as jnp
import numpy as np
from jax import lax
from jax.experimental import pallas as pl
from jax.experimental.pallas import tpu as pltpu
from jax.sharding import PartitionSpec as P

CH, SAMP, HALF, LAGS = 48, 256, 32, 65
CLU, STA = ("y", "xl", "core"), ("z", "xh")
N = 288
LO, EXTRA = 128, 17
ROWS = 72
TALL = 40
EI, EJ = 68, 69


def tables():
    u = np.arange(SAMP)[:, None]
    k = np.arange(N // 2 + 1)[None, :]
    angle = 2 * math.pi * ((u * k) % N) / N
    c, s = np.cos(angle), np.sin(angle)
    ch, sh = c[:, LO:], s[:, LO:]
    pad = np.zeros((SAMP, 128 - 4 * EXTRA))
    left = np.concatenate([c[:, :LO], s[:, :LO], ch, sh, sh, ch, pad], axis=1)
    right = np.concatenate([c[:, :LO], s[:, :LO], ch, sh, ch, sh, pad], axis=1)
    lag = np.arange(LAGS)[:, None] - HALF
    angle = 2 * math.pi * ((lag * k) % N) / N
    weight = np.where((k == 0) | (k == N // 2), 1.0, 2.0) / N
    c, s = np.cos(angle) * weight, np.sin(angle) * weight
    back = np.zeros((ROWS, 384))
    back[:LAGS, :LO] = c[:, :LO]
    back[:LAGS, LO:2 * LO] = -s[:, :LO]
    ch, sh = c[:, LO:], s[:, LO:]
    back[:LAGS, 256:256 + 4 * EXTRA] = np.concatenate([ch, ch, -sh, sh], axis=1)
    back[LAGS, 256 + EI] = 1.0
    back[LAGS + 1, 256 + EJ] = 1.0

    def split(t, axis):
        t = t.astype(np.float32)
        hi = t.astype(jnp.bfloat16)
        lo = (t - hi.astype(np.float32)).astype(jnp.bfloat16)
        return np.concatenate([hi, lo], axis=axis)

    return split(left, 1), split(right, 1), split(back, 0)


def spectrum(x, table, energy_lane, one_lane):
    d = jnp.dot(x, table, preferred_element_type=jnp.float32)
    d = d[:, :384] + d[:, 384:]
    xf = x.astype(jnp.float32)
    energy = jnp.sum(xf * xf, axis=1, keepdims=True)
    lane = lax.broadcasted_iota(jnp.int32, (1, 128), 1)
    third = jnp.where(lane == energy_lane, energy, d[:, 256:])
    third = jnp.where(lane == one_lane, 1.0, third)
    return d[:, :128], d[:, 128:256], third


def place():
    x, core = lax.axis_index("xl"), lax.axis_index("core")
    return lax.axis_index("y"), x * 2 + core, x, core


def pack_kernel(rows_ref, cube_ref, local_ref, remote_ref, *refs):
    parts, (own_ref, core_ref, chip_ref, lists_ref, sems) = refs[:4], refs[4:]
    row, step, _, _ = place()
    quarter = parts[0].shape[0]
    cuts = [
        pltpu.make_async_copy(rows_ref.at[pl.ds(pl.multiple_of(((row + d) & 3) * quarter, quarter), quarter)], out, sems.at[d])
        for d, out in enumerate(parts)
    ]
    channels, _, width = cube_ref.shape
    size = cube_ref.shape[1] // 4
    outs = (own_ref, core_ref, chip_ref.at[0], chip_ref.at[1])
    first = [pltpu.make_async_copy(ref.at[0], lists_ref.at[n], sems.at[4 + n]) for n, ref in enumerate((local_ref, remote_ref))]
    copies = []
    for d, out in enumerate(outs):
        at = pl.multiple_of((step ^ d) * size, size)
        for c in range(channels):
            copies.append(pltpu.make_async_copy(
                cube_ref.at[c, pl.ds(at, size)], out.at[pl.ds(c * size, size)], sems.at[6 + d * channels + c]
            ))
    for copy in first + cuts + copies:
        copy.start()
    for copy in first:
        copy.wait()
    line = lax.broadcasted_iota(jnp.int32, (16, width), 0)
    for d, out in enumerate(outs):
        lists = jnp.zeros((16, width), jnp.float32)
        for n in range(2):
            listed = lists_ref[n, pl.ds(step ^ d, 1), :].astype(jnp.float32)
            per = listed.shape[1] // width
            for k in range(per):
                lists = jnp.where(line == n * per + k, listed[:, k * width:(k + 1) * width], lists)
        out[pl.ds(channels * size, 16), :] = lists.astype(jnp.bfloat16)
    for copy in cuts + copies:
        copy.wait()


def pick_kernel(owners_ref, g0, g1, g2, g3, give_ref):
    row, step, _, _ = place()
    for d in (1, 3):
        behind = (row + 4 - (owners_ref[step ^ d] >> 2)) & 3
        for n, ref in enumerate((g0, g1, g2, g3)):

            @pl.when(behind == n)
            def _():
                give_ref[d // 2] = ref[...]


def core_kernel(owners_ref, g0, g1, g2, g3, got_ref, _, mine_0, mine_1, theirs_0, theirs_1):
    row, step, _, core = place()
    size = mine_0.shape[0]
    for d, outs in ((0, (mine_0, mine_1)), (2, (theirs_0, theirs_1))):
        owner = owners_ref[step ^ d]
        here = (owner & 1) == core
        behind = jnp.where(here, (row + 4 - (owner >> 2)) & 3, 4)
        for n, ref in enumerate((g0, g1, g2, g3, got_ref.at[d // 2])):

            @pl.when(behind == n)
            def _():
                for k, to in enumerate(outs):
                    to[...] = ref[pl.ds(k * size, size), :]


def chip_kernel(owners_ref, mine_ref, got_ref, out_ref):
    _, step, x, _ = place()
    here = ((owners_ref[step] >> 1) & 1) == x

    @pl.when(here)
    def _():
        out_ref[...] = mine_ref[...]

    @pl.when(jnp.logical_not(here))
    def _():
        out_ref[...] = got_ref[...]


def clear_rest(out_ref, channels):
    events = out_ref.shape[0] // 24
    for k in range(3):
        for c in range(channels, 8):
            out_ref[pl.ds(k * 8 + c, events, stride=24), :] = jnp.zeros((events, 128), jnp.float32)


def left_kernel(table_ref, b0, b1, b2, b3, out_ref):
    events = out_ref.shape[0] // 24 // 4
    channels = b0.shape[0] // events
    clear_rest(out_ref, channels)
    for q, w_ref in enumerate((b0, b1, b2, b3)):
        parts = spectrum(w_ref[:channels * events], table_ref[...], EI, EJ)
        for c in range(channels):
            for n, part in enumerate(parts):
                to = pl.ds(q * events * 24 + n * 8 + c, events, stride=24)
                out_ref[to, :] = part[c * events:(c + 1) * events]


def right_kernel(table_ref, *refs):
    pieces, out_ref = refs[:-1], refs[-1]
    events = out_ref.shape[0] // 24
    size = pieces[0].shape[0]
    clear_rest(out_ref, len(pieces) * size // events)
    row = place()[0]
    for n, p_ref in enumerate(pieces):
        base = (((row + 4 - (0, 1, 3, 2)[n % 4]) & 3) * 2 + n // 4) * size
        x = p_ref[...]
        parts = spectrum(x, table_ref[...], EJ, EI)
        for g in range(x.shape[0] // 32):
            at = base + 32 * g
            c = at // events
            to = (at - c * events) * 24 + c
            for k, part in enumerate(parts):
                out_ref[pl.ds(to + 8 * k, 32, stride=24), :] = part[32 * g:32 * g + 32]


def channel_sum(vs, sub):
    for shift in (4, 2, 1):
        keep = (sub & shift) == 0
        half = len(vs) // 2
        couples = list(zip(vs[:half], vs[half:]))
        if shift == 4:
            vs = [jnp.where(keep, a, b) + pltpu.roll(jnp.where(keep, b, a), 4, 0) for a, b in couples]
        else:
            vs = [jnp.where(keep, a + pltpu.roll(a, 8 - shift, 0), b + pltpu.roll(b, shift, 0)) for a, b in couples]
    return vs[0]


MOVES = (2, 1, 3, 0)


def target(k, dz, dh, count):
    return ((k // 2 + dz) % (count // 2)) * 2 + (k % 2 + dh) % 2


def pair_kernel(across, token_ref, local_ref, remote_ref, left, right, back_ref, out_ref, next_ref, z):
    width = out_ref.shape[2]
    half = out_ref.shape[0]
    next_ref[0] = token_ref[0]
    sta = lax.axis_index(STA)
    share = width // 4
    pairs = local_ref.shape[0] // 4
    back = back_ref[...]
    contract = (((1,), (1,)), ((), ()))
    dot = lambda a, b: lax.dot_general(a, b, contract, preferred_element_type=jnp.float32)
    sub = lax.broadcasted_iota(jnp.int32, (8, 128), 0)
    for t in range(half):
        first = target(sta, MOVES[t], across, 2 * half) * share

        def body(it, carry):
            sums = []
            for part in range(8):
                g = it * 8 + part
                q = g >> 3
                at = q * pairs + first + (g & 7) * 8
                products = [[], [], []]
                for p in range(8):
                    i = pl.multiple_of(local_ref[at + p], 8)
                    j = pl.multiple_of(remote_ref[at + p], 8)
                    xa, xb, xc = left[pl.ds(i, 8)], left[pl.ds(i + 8, 8)], left[pl.ds(i + 16, 8)]
                    ya, yb, yc = right[pl.ds(j, 8)], right[pl.ds(j + 8, 8)], right[pl.ds(j + 16, 8)]
                    for col, v in enumerate((xa * ya + xb * yb, xb * ya - xa * yb, xc * yc)):
                        products[col].append(v)
                sums += [(g, col, channel_sum(products[col], sub)) for col in range(3)]
            for g, col, v in sums:
                z[pl.ds(pl.multiple_of(g * 8, 8), 8), col * 128:col * 128 + 128] = v
            return carry

        lax.fori_loop(0, width // 64, body, 0)
        zk = z[...]
        zh = zk.astype(jnp.bfloat16)
        zl = (zk - zh.astype(jnp.float32)).astype(jnp.bfloat16)
        high = dot(back, zh)
        out_ref[t] = high[:ROWS] + high[ROWS:] + dot(back[:ROWS], zl)


def add_kernel(a_ref, b_ref, out_ref):
    z, step = lax.axis_index("z"), place()[1]
    share = a_ref.shape[2] // 4
    for t, dz in enumerate(MOVES):
        total = a_ref[t] + b_ref[t]
        for q in range(4):
            part = total[:, q * share:(q + 1) * share]
            slot = ((z + dz) & 3) * 4 + (step ^ q)
            out_ref[slot, :, :share] = part[:TALL]
            out_ref[slot, :ROWS - TALL, share:] = part[TALL:]


def final_kernel(near_ref, got_ref, out_ref):
    share = out_ref.shape[2]
    count = CH * SAMP
    for s in range(4):
        total = (got_ref[s] + got_ref[4 + s]) + (got_ref[8 + s] + got_ref[12 + s])
        total = jnp.concatenate([total[:, :share], total[:ROWS - TALL, share:]], axis=0)
        ni = 1.0 / jnp.sqrt(total[LAGS:LAGS + 1] / count + 1e-6)
        nj = 1.0 / jnp.sqrt(total[LAGS + 1:LAGS + 2] / count + 1e-6)
        out_ref[0, s] = (total * (ni * nj / count * near_ref[0, s].astype(jnp.float32))).T[:, :LAGS]


HBM = pl.BlockSpec(memory_space=pltpu.HBM)
ANY = pl.BlockSpec(memory_space=pl.ANY)
SMEM = pl.BlockSpec(memory_space=pltpu.SMEM)
VMEM = pl.BlockSpec(memory_space=pltpu.VMEM)
PARAMS = pltpu.CompilerParams(vmem_limit_bytes=20 * 1024 * 1024)
SMALL = pltpu.CompilerParams(vmem_limit_bytes=8 * 1024 * 1024)


def in_hbm(v):
    return pltpu.with_memory_space_constraint(v, pltpu.HBM)


def local(waves, owners, neighbours, pair_local, pair_remote):
    ev, ch, samp = waves.shape
    steps = owners.shape[0]
    pairs = pair_local.shape[2]
    n_clu, n_sta = lax.axis_size(CLU), lax.axis_size(STA)
    share = pairs // n_sta
    block = ev // steps
    left_table, right_table, back_table = (jnp.asarray(t) for t in tables())
    cube = waves.transpose(1, 0, 2)
    rows = cube.reshape(ch * ev, samp)
    f32, bf16 = jnp.float32, jnp.bfloat16
    shaped = jax.ShapeDtypeStruct

    me = lax.axis_index(CLU)
    row, step = me // 4, me % 4
    near = lambda v, d: v if d == 0 else lax.ppermute(v, CLU, [(i, i ^ d) for i in range(n_clu)])
    turn = lambda v, d: lax.ppermute(v, CLU, [(i, (i + 4 * d) % n_clu) for i in range(n_clu)])

    quarter = ch * ev // 4
    piece = shaped((quarter, samp), bf16)
    height = ch * block + 16
    payload = shaped((height, samp), bf16)
    *parts, own, core, chip = pl.pallas_call(
        pack_kernel, out_shape=(piece,) * 4 + (payload, payload, shaped((2, height, samp), bf16)),
        in_specs=[HBM] * 4, out_specs=(VMEM,) * 7,
        scratch_shapes=[pltpu.VMEM((2, steps, pairs), jnp.int32), pltpu.SemaphoreType.DMA((6 + 4 * ch,))],
        compiler_params=SMALL, name="pack",
    )(in_hbm(rows), in_hbm(cube), in_hbm(pair_local), in_hbm(pair_remote))
    chip = near(chip, 2)
    blocks = [own, near(core, 1), chip[0], near(chip[1], 1)]
    got = [part if d == 0 else turn(part, d) for d, part in enumerate(parts)]
    give = pl.pallas_call(
        pick_kernel, out_shape=shaped((2, quarter, samp), bf16), in_specs=[SMEM] + [VMEM] * 4, out_specs=VMEM,
        compiler_params=SMALL, name="pick",
    )(in_hbm(owners), *got)
    part = shaped((quarter // 2, samp), bf16)
    *mine, theirs_0, theirs_1 = pl.pallas_call(
        core_kernel, out_shape=(part,) * 4, in_specs=[SMEM] + [VMEM] * 5 + [ANY], out_specs=(VMEM,) * 4,
        compiler_params=SMALL, name="over_core",
    )(in_hbm(owners), *got, near(give, 1), chip)
    pieces = []
    for kept, sent in zip(mine, [near(theirs_0, 2), near(theirs_1, 2)]):
        whole = pl.pallas_call(
            chip_kernel, out_shape=part, in_specs=[SMEM] + [VMEM] * 2, out_specs=VMEM,
            compiler_params=SMALL, name="over_x",
        )(in_hbm(owners), kept, sent)
        pieces += [whole] + [turn(whole, d) for d in (1, -1, 2)]

    listed = jnp.stack([b[ch * block:ch * block + 2 * pairs // samp] for b in blocks]).astype(jnp.int32)
    listed = listed.reshape(4, 2, pairs) * 24
    first = listed[:, 0] + jnp.arange(4, dtype=jnp.int32)[:, None] * (block * 24)
    first, second = first.reshape(4 * pairs), listed[:, 1].reshape(4 * pairs)

    spectra = shaped((ev * 24, 128), f32)
    cost = pl.CostEstimate(flops=2 * ch * ev * samp * 768, bytes_accessed=4000000, transcendentals=0)
    left = pl.pallas_call(
        left_kernel, out_shape=spectra, in_specs=[VMEM] * 5, out_specs=VMEM,
        compiler_params=PARAMS, name="left", cost_estimate=cost,
    )(left_table, *blocks)
    right = pl.pallas_call(
        right_kernel, out_shape=spectra, in_specs=[VMEM] * (1 + len(pieces)), out_specs=VMEM,
        compiler_params=PARAMS, name="right", cost_estimate=cost,
    )(right_table, *pieces)

    halves = []
    token = owners
    for across in (1, 0):
        raw, token = pl.pallas_call(
            functools.partial(pair_kernel, across),
            out_shape=(shaped((n_sta // 2, ROWS, 4 * share), f32), shaped((steps,), jnp.int32)),
            in_specs=[SMEM] * 3 + [VMEM] * 3, out_specs=(VMEM, SMEM),
            scratch_shapes=[pltpu.VMEM((4 * share, 384), f32)],
            compiler_params=PARAMS, name="pairs", cost_estimate=cost,
        )(token, first, second, left, right, back_table)
        halves.append(raw)
    hop = lambda v, dz, dh: lax.ppermute(v, STA, [(k, target(k, dz, dh, n_sta)) for k in range(n_sta)])
    slots = pl.pallas_call(
        add_kernel, out_shape=shaped((2 * n_sta, TALL, 2 * share), f32), in_specs=[VMEM] * 2, out_specs=VMEM,
        compiler_params=SMALL, name="add",
    )(hop(halves[0], 0, 1), halves[1])
    slots = lax.all_to_all(slots, ("z", "xl", "core"), 0, 0)
    out = pl.pallas_call(
        final_kernel, out_shape=shaped((1, steps, share, LAGS), f32),
        in_specs=[SMEM, VMEM], out_specs=VMEM, compiler_params=SMALL, name="finish",
    )(neighbours, slots)
    return out.transpose(0, 1, 3, 2)


def solution(mesh):
    fine = jax.sharding.Mesh(mesh.devices.reshape(4, 2, 2, 4, 2), CLU + STA)
    placed = (
        P(CLU, STA, None),
        P(),
        P(CLU, None),
        P(CLU, None, None),
        P(CLU, None, None),
    )
    return jax.shard_map(
        local, mesh=fine, in_specs=placed, out_specs=P(CLU, None, None, STA), check_vma=False
    )
```

```python
import math

import jax
import jax.numpy as jnp
import numpy as np
from jax import lax
from jax.experimental import pallas as pl
from jax.experimental.pallas import tpu as pltpu
from jax.sharding import PartitionSpec as P

CH, SAMP, HALF, LAGS = 48, 256, 32, 65
CLU, STA = ("y", "xl", "core"), ("z", "xh")
N = 288
LO, EXTRA = 128, 17
ROWS = 72
TALL = 40
EI, EJ = 68, 69


def tables():
    u = np.arange(SAMP)[:, None]
    k = np.arange(N // 2 + 1)[None, :]
    angle = 2 * math.pi * ((u * k) % N) / N
    c, s = np.cos(angle), np.sin(angle)
    ch, sh = c[:, LO:], s[:, LO:]
    pad = np.zeros((SAMP, 128 - 4 * EXTRA))
    left = np.concatenate([c[:, :LO], s[:, :LO], ch, sh, sh, ch, pad], axis=1)
    right = np.concatenate([c[:, :LO], s[:, :LO], ch, sh, ch, sh, pad], axis=1)
    lag = np.arange(LAGS)[:, None] - HALF
    angle = 2 * math.pi * ((lag * k) % N) / N
    weight = np.where((k == 0) | (k == N // 2), 1.0, 2.0) / N
    c, s = np.cos(angle) * weight, np.sin(angle) * weight
    back = np.zeros((ROWS, 384))
    back[:LAGS, :LO] = c[:, :LO]
    back[:LAGS, LO:2 * LO] = -s[:, :LO]
    ch, sh = c[:, LO:], s[:, LO:]
    back[:LAGS, 256:256 + 4 * EXTRA] = np.concatenate([ch, ch, -sh, sh], axis=1)
    back[LAGS, 256 + EI] = 1.0
    back[LAGS + 1, 256 + EJ] = 1.0

    def split(t, axis):
        t = t.astype(np.float32)
        hi = t.astype(jnp.bfloat16)
        lo = (t - hi.astype(np.float32)).astype(jnp.bfloat16)
        return np.concatenate([hi, lo], axis=axis)

    return split(left, 1), split(right, 1), split(back, 0)


def spectrum(x, table, energy_lane, one_lane):
    d = jnp.dot(x, table, preferred_element_type=jnp.float32)
    d = d[:, :384] + d[:, 384:]
    xf = x.astype(jnp.float32)
    energy = jnp.sum(xf * xf, axis=1, keepdims=True)
    lane = lax.broadcasted_iota(jnp.int32, (1, 128), 1)
    third = jnp.where(lane == energy_lane, energy, d[:, 256:])
    third = jnp.where(lane == one_lane, 1.0, third)
    return d[:, :128], d[:, 128:256], third


def place():
    x, core = lax.axis_index("xl"), lax.axis_index("core")
    return lax.axis_index("y"), x * 2 + core, x, core


def pack_kernel(rows_ref, cube_ref, local_ref, remote_ref, *refs):
    parts, (own_ref, core_ref, chip_ref, lists_ref, sems) = refs[:4], refs[4:]
    row, step, _, _ = place()
    quarter = parts[0].shape[0]
    cuts = [
        pltpu.make_async_copy(rows_ref.at[pl.ds(pl.multiple_of(((row + d) & 3) * quarter, quarter), quarter)], out, sems.at[d])
        for d, out in enumerate(parts)
    ]
    channels, _, width = cube_ref.shape
    size = cube_ref.shape[1] // 4
    outs = (own_ref, core_ref, chip_ref.at[0], chip_ref.at[1])
    first = [pltpu.make_async_copy(ref.at[0], lists_ref.at[n], sems.at[4 + n]) for n, ref in enumerate((local_ref, remote_ref))]
    copies = []
    for d, out in enumerate(outs):
        at = pl.multiple_of((step ^ d) * size, size)
        for c in range(channels):
            copies.append(pltpu.make_async_copy(
                cube_ref.at[c, pl.ds(at, size)], out.at[pl.ds(c * size, size)], sems.at[6 + d * channels + c]
            ))
    for copy in first + cuts + copies:
        copy.start()
    for copy in first:
        copy.wait()
    line = lax.broadcasted_iota(jnp.int32, (16, width), 0)
    for d, out in enumerate(outs):
        lists = jnp.zeros((16, width), jnp.float32)
        for n in range(2):
            listed = lists_ref[n, pl.ds(step ^ d, 1), :].astype(jnp.float32)
            per = listed.shape[1] // width
            for k in range(per):
                lists = jnp.where(line == n * per + k, listed[:, k * width:(k + 1) * width], lists)
        out[pl.ds(channels * size, 16), :] = lists.astype(jnp.bfloat16)
    for copy in cuts + copies:
        copy.wait()


def pick_kernel(owners_ref, g0, g1, g2, g3, give_ref):
    row, step, _, _ = place()
    for d in (1, 3):
        behind = (row + 4 - (owners_ref[step ^ d] >> 2)) & 3
        for n, ref in enumerate((g0, g1, g2, g3)):

            @pl.when(behind == n)
            def _():
                give_ref[d // 2] = ref[...]


def core_kernel(owners_ref, g0, g1, g2, g3, got_ref, _, mine_0, mine_1, theirs_0, theirs_1):
    row, step, _, core = place()
    size = mine_0.shape[0]
    for d, outs in ((0, (mine_0, mine_1)), (2, (theirs_0, theirs_1))):
        owner = owners_ref[step ^ d]
        here = (owner & 1) == core
        behind = jnp.where(here, (row + 4 - (owner >> 2)) & 3, 4)
        for n, ref in enumerate((g0, g1, g2, g3, got_ref.at[d // 2])):

            @pl.when(behind == n)
            def _():
                for k, to in enumerate(outs):
                    to[...] = ref[pl.ds(k * size, size), :]


def chip_kernel(owners_ref, mine_ref, got_ref, out_ref):
    _, step, x, _ = place()
    here = ((owners_ref[step] >> 1) & 1) == x

    @pl.when(here)
    def _():
        out_ref[...] = mine_ref[...]

    @pl.when(jnp.logical_not(here))
    def _():
        out_ref[...] = got_ref[...]


def clear_rest(out_ref, channels):
    events = out_ref.shape[0] // 24
    for k in range(3):
        for c in range(channels, 8):
            out_ref[pl.ds(k * 8 + c, events, stride=24), :] = jnp.zeros((events, 128), jnp.float32)


def left_kernel(table_ref, b0, b1, b2, b3, _, out_ref):
    events = out_ref.shape[0] // 24 // 4
    channels = b0.shape[0] // events
    clear_rest(out_ref, channels)
    for q, w_ref in enumerate((b0, b1, b2, b3)):
        parts = spectrum(w_ref[:channels * events], table_ref[...], EI, EJ)
        for c in range(channels):
            for n, part in enumerate(parts):
                to = pl.ds(q * events * 24 + n * 8 + c, events, stride=24)
                out_ref[to, :] = part[c * events:(c + 1) * events]


def right_spectra(table_ref, pieces, out_ref):
    events = out_ref.shape[0] // 24
    size = pieces[0].shape[0]
    clear_rest(out_ref, len(pieces) * size // events)
    row = place()[0]
    for n, p_ref in enumerate(pieces):
        base = (((row + 4 - (0, 1, 3, 2)[n % 4]) & 3) * 2 + n // 4) * size
        x = p_ref[...]
        parts = spectrum(x, table_ref[...], EJ, EI)
        for g in range(x.shape[0] // 32):
            at = base + 32 * g
            c = at // events
            to = (at - c * events) * 24 + c
            for k, part in enumerate(parts):
                out_ref[pl.ds(to + 8 * k, 32, stride=24), :] = part[32 * g:32 * g + 32]


def channel_sum(vs, sub):
    for shift in (4, 2, 1):
        keep = (sub & shift) == 0
        half = len(vs) // 2
        couples = list(zip(vs[:half], vs[half:]))
        if shift == 4:
            vs = [jnp.where(keep, a, b) + pltpu.roll(jnp.where(keep, b, a), 4, 0) for a, b in couples]
        else:
            vs = [jnp.where(keep, a + pltpu.roll(a, 8 - shift, 0), b + pltpu.roll(b, shift, 0)) for a, b in couples]
    return vs[0]


MOVES = (2, 1, 3, 0)


def target(k, dz, dh, count):
    return ((k // 2 + dz) % (count // 2)) * 2 + (k % 2 + dh) % 2


def first_kernel(lists_ref, left, back_ref, table_ref, *refs):
    pieces, (out_ref, right, z) = refs[:-3], refs[-3:]
    right_spectra(table_ref, pieces, right)
    pair_products(1, lists_ref, left, right, back_ref, out_ref, z)


def second_kernel(lists_ref, left, back_ref, right, _, out_ref, z):
    pair_products(0, lists_ref, left, right, back_ref, out_ref, z)


def pair_products(across, lists_ref, left, right, back_ref, out_ref, z):
    width = out_ref.shape[2]
    half = out_ref.shape[0]
    sta = lax.axis_index(STA)
    share = width // 4
    pairs = lists_ref.shape[0] // 8
    back = back_ref[...]
    contract = (((1,), (1,)), ((), ()))
    dot = lambda a, b: lax.dot_general(a, b, contract, preferred_element_type=jnp.float32)
    sub = lax.broadcasted_iota(jnp.int32, (8, 128), 0)
    for t in range(half):
        first = target(sta, MOVES[t], across, 2 * half) * share

        def body(it, carry):
            sums = []
            for part in range(8):
                g = it * 8 + part
                q = g >> 3
                at = q * pairs + first + (g & 7) * 8
                products = [[], [], []]
                for p in range(8):
                    i = pl.multiple_of(lists_ref[at + p], 8)
                    j = pl.multiple_of(lists_ref[at + 4 * pairs + p], 8)
                    xa, xb, xc = left[pl.ds(i, 8)], left[pl.ds(i + 8, 8)], left[pl.ds(i + 16, 8)]
                    ya, yb, yc = right[pl.ds(j, 8)], right[pl.ds(j + 8, 8)], right[pl.ds(j + 16, 8)]
                    for col, v in enumerate((xa * ya + xb * yb, xb * ya - xa * yb, xc * yc)):
                        products[col].append(v)
                sums += [(g, col, channel_sum(products[col], sub)) for col in range(3)]
            for g, col, v in sums:
                z[pl.ds(pl.multiple_of(g * 8, 8), 8), col * 128:col * 128 + 128] = v
            return carry

        lax.fori_loop(0, width // 64, body, 0)
        zk = z[...]
        zh = zk.astype(jnp.bfloat16)
        zl = (zk - zh.astype(jnp.float32)).astype(jnp.bfloat16)
        high = dot(back, zh)
        out_ref[t] = high[:ROWS] + high[ROWS:] + dot(back[:ROWS], zl)


def add_kernel(a_ref, b_ref, out_ref):
    z, step = lax.axis_index("z"), place()[1]
    share = a_ref.shape[2] // 4
    for t, dz in enumerate(MOVES):
        total = a_ref[t] + b_ref[t]
        for q in range(4):
            part = total[:, q * share:(q + 1) * share]
            slot = ((z + dz) & 3) * 4 + (step ^ q)
            out_ref[slot, :, :share] = part[:TALL]
            out_ref[slot, :ROWS - TALL, share:] = part[TALL:]


def final_kernel(near_ref, got_ref, out_ref):
    share = out_ref.shape[2]
    count = CH * SAMP
    for s in range(4):
        total = (got_ref[s] + got_ref[4 + s]) + (got_ref[8 + s] + got_ref[12 + s])
        total = jnp.concatenate([total[:, :share], total[:ROWS - TALL, share:]], axis=0)
        ni = 1.0 / jnp.sqrt(total[LAGS:LAGS + 1] / count + 1e-6)
        nj = 1.0 / jnp.sqrt(total[LAGS + 1:LAGS + 2] / count + 1e-6)
        out_ref[0, s] = (total * (ni * nj / count * near_ref[0, s].astype(jnp.float32))).T[:, :LAGS]


HBM = pl.BlockSpec(memory_space=pltpu.HBM)
ANY = pl.BlockSpec(memory_space=pl.ANY)
SMEM = pl.BlockSpec(memory_space=pltpu.SMEM)
VMEM = pl.BlockSpec(memory_space=pltpu.VMEM)
PARAMS = pltpu.CompilerParams(vmem_limit_bytes=20 * 1024 * 1024)
SMALL = pltpu.CompilerParams(vmem_limit_bytes=8 * 1024 * 1024)


def in_hbm(v):
    return pltpu.with_memory_space_constraint(v, pltpu.HBM)


def local(waves, owners, neighbours, pair_local, pair_remote):
    ev, ch, samp = waves.shape
    steps = owners.shape[0]
    pairs = pair_local.shape[2]
    n_clu, n_sta = lax.axis_size(CLU), lax.axis_size(STA)
    share = pairs // n_sta
    block = ev // steps
    left_table, right_table, back_table = (jnp.asarray(t) for t in tables())
    cube = waves.transpose(1, 0, 2)
    rows = cube.reshape(ch * ev, samp)
    f32, bf16 = jnp.float32, jnp.bfloat16
    shaped = jax.ShapeDtypeStruct

    me = lax.axis_index(CLU)
    row, step = me // 4, me % 4
    near = lambda v, d: v if d == 0 else lax.ppermute(v, CLU, [(i, i ^ d) for i in range(n_clu)])
    turn = lambda v, d: lax.ppermute(v, CLU, [(i, (i + 4 * d) % n_clu) for i in range(n_clu)])

    quarter = ch * ev // 4
    piece = shaped((quarter, samp), bf16)
    height = ch * block + 16
    payload = shaped((height, samp), bf16)
    *parts, own, core, chip = pl.pallas_call(
        pack_kernel, out_shape=(piece,) * 4 + (payload, payload, shaped((2, height, samp), bf16)),
        in_specs=[HBM] * 4, out_specs=(VMEM,) * 7,
        scratch_shapes=[pltpu.VMEM((2, steps, pairs), jnp.int32), pltpu.SemaphoreType.DMA((6 + 4 * ch,))],
        compiler_params=SMALL, name="pack",
    )(in_hbm(rows), in_hbm(cube), in_hbm(pair_local), in_hbm(pair_remote))
    chip = near(chip, 2)
    blocks = [own, near(core, 1), chip[0], near(chip[1], 1)]
    got = [part if d == 0 else turn(part, d) for d, part in enumerate(parts)]
    give = pl.pallas_call(
        pick_kernel, out_shape=shaped((2, quarter, samp), bf16), in_specs=[SMEM] + [VMEM] * 4, out_specs=VMEM,
        compiler_params=SMALL, name="pick",
    )(in_hbm(owners), *got)
    part = shaped((quarter // 2, samp), bf16)
    *mine, theirs_0, theirs_1 = pl.pallas_call(
        core_kernel, out_shape=(part,) * 4, in_specs=[SMEM] + [VMEM] * 5 + [ANY], out_specs=(VMEM,) * 4,
        compiler_params=SMALL, name="over_core",
    )(in_hbm(owners), *got, near(give, 1), chip)
    pieces = []
    for kept, sent in zip(mine, [near(theirs_0, 2), near(theirs_1, 2)]):
        whole = pl.pallas_call(
            chip_kernel, out_shape=part, in_specs=[SMEM] + [VMEM] * 2, out_specs=VMEM,
            compiler_params=SMALL, name="over_x",
        )(in_hbm(owners), kept, sent)
        pieces += [whole] + [turn(whole, d) for d in (1, -1, 2)]

    listed = jnp.stack([b[ch * block:ch * block + 2 * pairs // samp] for b in blocks]).astype(jnp.int32)
    listed = listed.reshape(4, 2, pairs) * 24
    first = listed[:, 0] + jnp.arange(4, dtype=jnp.int32)[:, None] * (block * 24)
    lists = jnp.concatenate([first.reshape(4 * pairs), listed[:, 1].reshape(4 * pairs)])

    spectra = shaped((ev * 24, 128), f32)
    cost = pl.CostEstimate(flops=2 * ch * ev * samp * 768, bytes_accessed=4000000, transcendentals=0)
    left = pl.pallas_call(
        left_kernel, out_shape=spectra, in_specs=[VMEM] * 5 + [ANY], out_specs=VMEM,
        compiler_params=PARAMS, name="left", cost_estimate=cost,
    )(left_table, *blocks, pieces[1])
    raw = shaped((n_sta // 2, ROWS, 4 * share), f32)
    products = pltpu.VMEM((4 * share, 384), f32)
    far, right = pl.pallas_call(
        first_kernel, out_shape=(raw, spectra), in_specs=[SMEM] + [VMEM] * (3 + len(pieces)), out_specs=(VMEM,) * 2,
        scratch_shapes=[products], compiler_params=PARAMS, name="first", cost_estimate=cost,
    )(lists, left, back_table, right_table, *pieces)
    here = pl.pallas_call(
        second_kernel, out_shape=raw, in_specs=[SMEM] + [VMEM] * 3 + [ANY], out_specs=VMEM,
        scratch_shapes=[products], compiler_params=PARAMS, name="second", cost_estimate=cost,
    )(lists, left, back_table, right, far)
    hop = lambda v, dz, dh: lax.ppermute(v, STA, [(k, target(k, dz, dh, n_sta)) for k in range(n_sta)])
    slots = pl.pallas_call(
        add_kernel, out_shape=shaped((2 * n_sta, TALL, 2 * share), f32), in_specs=[VMEM] * 2, out_specs=VMEM,
        compiler_params=SMALL, name="add",
    )(hop(far, 0, 1), here)
    slots = lax.all_to_all(slots, ("z", "xl", "core"), 0, 0)
    out = pl.pallas_call(
        final_kernel, out_shape=shaped((1, steps, share, LAGS), f32),
        in_specs=[SMEM, VMEM], out_specs=VMEM, compiler_params=SMALL, name="finish",
    )(neighbours, slots)
    return out.transpose(0, 1, 3, 2)


def solution(mesh):
    fine = jax.sharding.Mesh(mesh.devices.reshape(4, 2, 2, 4, 2), CLU + STA)
    placed = (
        P(CLU, STA, None),
        P(),
        P(CLU, None),
        P(CLU, None, None),
        P(CLU, None, None),
    )
    return jax.shard_map(
        local, mesh=fine, in_specs=placed, out_specs=P(CLU, None, None, STA), check_vma=False
    )
```

```python
import functools
import math

import jax
import jax.numpy as jnp
import numpy as np
from jax import lax
from jax.experimental import pallas as pl
from jax.experimental.pallas import tpu as pltpu
from jax.sharding import PartitionSpec as P

CH, SAMP, HALF, LAGS = 48, 256, 32, 65
CLU, STA = ("y", "xl", "core"), ("z", "xh")
N = 288
LO, EXTRA = 128, 17
ROWS = 72
TALL = 40
EI, EJ = 68, 69


def tables():
    u = np.arange(SAMP)[:, None]
    k = np.arange(N // 2 + 1)[None, :]
    angle = 2 * math.pi * ((u * k) % N) / N
    c, s = np.cos(angle), np.sin(angle)
    ch, sh = c[:, LO:], s[:, LO:]
    pad = np.zeros((SAMP, 128 - 4 * EXTRA))
    left = np.concatenate([c[:, :LO], s[:, :LO], ch, sh, sh, ch, pad], axis=1)
    right = np.concatenate([c[:, :LO], s[:, :LO], ch, sh, ch, sh, pad], axis=1)
    lag = np.arange(LAGS)[:, None] - HALF
    angle = 2 * math.pi * ((lag * k) % N) / N
    weight = np.where((k == 0) | (k == N // 2), 1.0, 2.0) / N
    c, s = np.cos(angle) * weight, np.sin(angle) * weight
    back = np.zeros((ROWS, 384))
    back[:LAGS, :LO] = c[:, :LO]
    back[:LAGS, LO:2 * LO] = -s[:, :LO]
    ch, sh = c[:, LO:], s[:, LO:]
    back[:LAGS, 256:256 + 4 * EXTRA] = np.concatenate([ch, ch, -sh, sh], axis=1)
    back[LAGS, 256 + EI] = 1.0
    back[LAGS + 1, 256 + EJ] = 1.0

    def split(t, axis):
        t = t.astype(np.float32)
        hi = t.astype(jnp.bfloat16)
        lo = (t - hi.astype(np.float32)).astype(jnp.bfloat16)
        return np.concatenate([hi, lo], axis=axis)

    return split(left, 1), split(right, 1), split(back, 0)


def spectrum(x, table, energy_lane, one_lane):
    d = jnp.dot(x, table, preferred_element_type=jnp.float32)
    d = d[:, :384] + d[:, 384:]
    xf = x.astype(jnp.float32)
    energy = jnp.sum(xf * xf, axis=1, keepdims=True)
    lane = lax.broadcasted_iota(jnp.int32, (1, 128), 1)
    third = jnp.where(lane == energy_lane, energy, d[:, 256:])
    third = jnp.where(lane == one_lane, 1.0, third)
    return d[:, :128], d[:, 128:256], third


def place():
    x, core = lax.axis_index("xl"), lax.axis_index("core")
    return lax.axis_index("y"), x * 2 + core, x, core


def pack_kernel(rows_ref, cube_ref, local_ref, remote_ref, *refs):
    parts, (own_ref, core_ref, chip_ref, lists_ref, sems) = refs[:4], refs[4:]
    row, step, _, _ = place()
    quarter = parts[0].shape[0]
    cuts = [
        pltpu.make_async_copy(rows_ref.at[pl.ds(pl.multiple_of(((row + d) & 3) * quarter, quarter), quarter)], out, sems.at[d])
        for d, out in enumerate(parts)
    ]
    channels, _, width = cube_ref.shape
    size = cube_ref.shape[1] // 4
    outs = (own_ref, core_ref, chip_ref.at[0], chip_ref.at[1])
    first = [pltpu.make_async_copy(ref.at[0], lists_ref.at[n], sems.at[4 + n]) for n, ref in enumerate((local_ref, remote_ref))]
    copies = []
    for d, out in enumerate(outs):
        at = pl.multiple_of((step ^ d) * size, size)
        for c in range(channels):
            copies.append(pltpu.make_async_copy(
                cube_ref.at[c, pl.ds(at, size)], out.at[pl.ds(c * size, size)], sems.at[6 + d * channels + c]
            ))
    for copy in first + cuts + copies:
        copy.start()
    for copy in first:
        copy.wait()
    line = lax.broadcasted_iota(jnp.int32, (16, width), 0)
    for d, out in enumerate(outs):
        lists = jnp.zeros((16, width), jnp.float32)
        for n in range(2):
            listed = lists_ref[n, pl.ds(step ^ d, 1), :].astype(jnp.float32)
            per = listed.shape[1] // width
            for k in range(per):
                lists = jnp.where(line == n * per + k, listed[:, k * width:(k + 1) * width], lists)
        out[pl.ds(channels * size, 16), :] = lists.astype(jnp.bfloat16)
    for copy in cuts + copies:
        copy.wait()


def pick_kernel(owners_ref, g0, g1, g2, g3, give_ref):
    row, step, _, _ = place()
    for d in (1, 3):
        behind = (row + 4 - (owners_ref[step ^ d] >> 2)) & 3
        for n, ref in enumerate((g0, g1, g2, g3)):

            @pl.when(behind == n)
            def _():
                give_ref[d // 2] = ref[...]


def core_kernel(owners_ref, g0, g1, g2, g3, got_ref, _, mine_0, mine_1, theirs_0, theirs_1):
    row, step, _, core = place()
    size = mine_0.shape[0]
    for d, outs in ((0, (mine_0, mine_1)), (2, (theirs_0, theirs_1))):
        owner = owners_ref[step ^ d]
        here = (owner & 1) == core
        behind = jnp.where(here, (row + 4 - (owner >> 2)) & 3, 4)
        for n, ref in enumerate((g0, g1, g2, g3, got_ref.at[d // 2])):

            @pl.when(behind == n)
            def _():
                for k, to in enumerate(outs):
                    to[...] = ref[pl.ds(k * size, size), :]


def chip_kernel(owners_ref, mine_ref, got_ref, out_ref):
    _, step, x, _ = place()
    here = ((owners_ref[step] >> 1) & 1) == x

    @pl.when(here)
    def _():
        out_ref[...] = mine_ref[...]

    @pl.when(jnp.logical_not(here))
    def _():
        out_ref[...] = got_ref[...]


def clear_rest(out_ref, channels):
    events = out_ref.shape[0] // 24
    for k in range(3):
        for c in range(channels, 8):
            out_ref[pl.ds(k * 8 + c, events, stride=24), :] = jnp.zeros((events, 128), jnp.float32)


def left_kernel(table_ref, b0, b1, b2, b3, out_ref):
    events = out_ref.shape[0] // 24 // 4
    channels = b0.shape[0] // events
    clear_rest(out_ref, channels)
    for q, w_ref in enumerate((b0, b1, b2, b3)):
        parts = spectrum(w_ref[:channels * events], table_ref[...], EI, EJ)
        for c in range(channels):
            for n, part in enumerate(parts):
                to = pl.ds(q * events * 24 + n * 8 + c, events, stride=24)
                out_ref[to, :] = part[c * events:(c + 1) * events]


def right_kernel(table_ref, *refs):
    pieces, out_ref = refs[:-1], refs[-1]
    events = out_ref.shape[0] // 24
    size = pieces[0].shape[0]
    clear_rest(out_ref, len(pieces) * size // events)
    row = place()[0]
    for n, p_ref in enumerate(pieces):
        base = (((row + 4 - (0, 1, 3, 2)[n % 4]) & 3) * 2 + n // 4) * size
        x = p_ref[...]
        parts = spectrum(x, table_ref[...], EJ, EI)
        for g in range(x.shape[0] // 32):
            at = base + 32 * g
            c = at // events
            to = (at - c * events) * 24 + c
            for k, part in enumerate(parts):
                out_ref[pl.ds(to + 8 * k, 32, stride=24), :] = part[32 * g:32 * g + 32]


def channel_sum(vs, sub):
    for shift in (4, 2, 1):
        keep = (sub & shift) == 0
        half = len(vs) // 2
        couples = list(zip(vs[:half], vs[half:]))
        if shift == 4:
            vs = [jnp.where(keep, a, b) + pltpu.roll(jnp.where(keep, b, a), 4, 0) for a, b in couples]
        else:
            vs = [jnp.where(keep, a + pltpu.roll(a, 8 - shift, 0), b + pltpu.roll(b, shift, 0)) for a, b in couples]
    return vs[0]


MOVES = (2, 1, 3, 0)


def target(k, dz, dh, count):
    return ((k // 2 + dz) % (count // 2)) * 2 + (k % 2 + dh) % 2


def pair_kernel(across, local_ref, remote_ref, left, right, back_ref, *refs):
    out_ref, z = refs[-2:]
    width = out_ref.shape[2]
    half = out_ref.shape[0]
    sta = lax.axis_index(STA)
    share = width // 4
    pairs = local_ref.shape[0] // 4
    back = back_ref[...]
    contract = (((1,), (1,)), ((), ()))
    dot = lambda a, b: lax.dot_general(a, b, contract, preferred_element_type=jnp.float32)
    sub = lax.broadcasted_iota(jnp.int32, (8, 128), 0)
    for t in range(half):
        first = target(sta, MOVES[t], across, 2 * half) * share

        def body(it, carry):
            sums = []
            for part in range(8):
                g = it * 8 + part
                q = g >> 3
                at = q * pairs + first + (g & 7) * 8
                products = [[], [], []]
                for p in range(8):
                    i = pl.multiple_of(local_ref[at + p], 8)
                    j = pl.multiple_of(remote_ref[at + p], 8)
                    xa, xb, xc = left[pl.ds(i, 8)], left[pl.ds(i + 8, 8)], left[pl.ds(i + 16, 8)]
                    ya, yb, yc = right[pl.ds(j, 8)], right[pl.ds(j + 8, 8)], right[pl.ds(j + 16, 8)]
                    for col, v in enumerate((xa * ya + xb * yb, xb * ya - xa * yb, xc * yc)):
                        products[col].append(v)
                sums += [(g, col, channel_sum(products[col], sub)) for col in range(3)]
            for g, col, v in sums:
                z[pl.ds(pl.multiple_of(g * 8, 8), 8), col * 128:col * 128 + 128] = v
            return carry

        lax.fori_loop(0, width // 64, body, 0)
        zk = z[...]
        zh = zk.astype(jnp.bfloat16)
        zl = (zk - zh.astype(jnp.float32)).astype(jnp.bfloat16)
        high = dot(back, zh)
        out_ref[t] = high[:ROWS] + high[ROWS:] + dot(back[:ROWS], zl)


def add_kernel(a_ref, b_ref, out_ref):
    z, step = lax.axis_index("z"), place()[1]
    share = a_ref.shape[2] // 4
    for t, dz in enumerate(MOVES):
        total = a_ref[t] + b_ref[t]
        for q in range(4):
            part = total[:, q * share:(q + 1) * share]
            slot = ((z + dz) & 3) * 4 + (step ^ q)
            out_ref[slot, :, :share] = part[:TALL]
            out_ref[slot, :ROWS - TALL, share:] = part[TALL:]


def final_kernel(near_ref, got_ref, out_ref):
    share = out_ref.shape[2]
    count = CH * SAMP
    for s in range(4):
        total = (got_ref[s] + got_ref[4 + s]) + (got_ref[8 + s] + got_ref[12 + s])
        total = jnp.concatenate([total[:, :share], total[:ROWS - TALL, share:]], axis=0)
        ni = 1.0 / jnp.sqrt(total[LAGS:LAGS + 1] / count + 1e-6)
        nj = 1.0 / jnp.sqrt(total[LAGS + 1:LAGS + 2] / count + 1e-6)
        out_ref[0, s] = (total * (ni * nj / count * near_ref[0, s].astype(jnp.float32))).T[:, :LAGS]


HBM = pl.BlockSpec(memory_space=pltpu.HBM)
ANY = pl.BlockSpec(memory_space=pl.ANY)
SMEM = pl.BlockSpec(memory_space=pltpu.SMEM)
VMEM = pl.BlockSpec(memory_space=pltpu.VMEM)
PARAMS = pltpu.CompilerParams(vmem_limit_bytes=20 * 1024 * 1024)
SMALL = pltpu.CompilerParams(vmem_limit_bytes=8 * 1024 * 1024)


def in_hbm(v):
    return pltpu.with_memory_space_constraint(v, pltpu.HBM)


def local(waves, owners, neighbours, pair_local, pair_remote):
    ev, ch, samp = waves.shape
    steps = owners.shape[0]
    pairs = pair_local.shape[2]
    n_clu, n_sta = lax.axis_size(CLU), lax.axis_size(STA)
    share = pairs // n_sta
    block = ev // steps
    left_table, right_table, back_table = (jnp.asarray(t) for t in tables())
    cube = waves.transpose(1, 0, 2)
    rows = cube.reshape(ch * ev, samp)
    f32, bf16 = jnp.float32, jnp.bfloat16
    shaped = jax.ShapeDtypeStruct

    me = lax.axis_index(CLU)
    row, step = me // 4, me % 4
    near = lambda v, d: v if d == 0 else lax.ppermute(v, CLU, [(i, i ^ d) for i in range(n_clu)])
    turn = lambda v, d: lax.ppermute(v, CLU, [(i, (i + 4 * d) % n_clu) for i in range(n_clu)])

    quarter = ch * ev // 4
    piece = shaped((quarter, samp), bf16)
    height = ch * block + 16
    payload = shaped((height, samp), bf16)
    *parts, own, core, chip = pl.pallas_call(
        pack_kernel, out_shape=(piece,) * 4 + (payload, payload, shaped((2, height, samp), bf16)),
        in_specs=[HBM] * 4, out_specs=(VMEM,) * 7,
        scratch_shapes=[pltpu.VMEM((2, steps, pairs), jnp.int32), pltpu.SemaphoreType.DMA((6 + 4 * ch,))],
        compiler_params=SMALL, name="pack",
    )(in_hbm(rows), in_hbm(cube), in_hbm(pair_local), in_hbm(pair_remote))
    chip = near(chip, 2)
    blocks = [own, near(core, 1), chip[0], near(chip[1], 1)]
    got = [part if d == 0 else turn(part, d) for d, part in enumerate(parts)]
    give = pl.pallas_call(
        pick_kernel, out_shape=shaped((2, quarter, samp), bf16), in_specs=[SMEM] + [VMEM] * 4, out_specs=VMEM,
        compiler_params=SMALL, name="pick",
    )(in_hbm(owners), *got)
    part = shaped((quarter // 2, samp), bf16)
    *mine, theirs_0, theirs_1 = pl.pallas_call(
        core_kernel, out_shape=(part,) * 4, in_specs=[SMEM] + [VMEM] * 5 + [ANY], out_specs=(VMEM,) * 4,
        compiler_params=SMALL, name="over_core",
    )(in_hbm(owners), *got, near(give, 1), chip)
    pieces = []
    for kept, sent in zip(mine, [near(theirs_0, 2), near(theirs_1, 2)]):
        whole = pl.pallas_call(
            chip_kernel, out_shape=part, in_specs=[SMEM] + [VMEM] * 2, out_specs=VMEM,
            compiler_params=SMALL, name="over_x",
        )(in_hbm(owners), kept, sent)
        pieces += [whole] + [turn(whole, d) for d in (1, -1, 2)]

    listed = jnp.stack([b[ch * block:ch * block + 2 * pairs // samp] for b in blocks]).astype(jnp.int32)
    listed = listed.reshape(4, 2, pairs) * 24
    first = listed[:, 0] + jnp.arange(4, dtype=jnp.int32)[:, None] * (block * 24)
    first, second = first.reshape(4 * pairs), listed[:, 1].reshape(4 * pairs)

    spectra = shaped((ev * 24, 128), f32)
    cost = pl.CostEstimate(flops=2 * ch * ev * samp * 768, bytes_accessed=4000000, transcendentals=0)
    left = pl.pallas_call(
        left_kernel, out_shape=spectra, in_specs=[VMEM] * 5, out_specs=VMEM,
        compiler_params=PARAMS, name="left", cost_estimate=cost,
    )(left_table, *blocks)
    right = pl.pallas_call(
        right_kernel, out_shape=spectra, in_specs=[VMEM] * (1 + len(pieces)), out_specs=VMEM,
        compiler_params=PARAMS, name="right", cost_estimate=cost,
    )(right_table, *pieces)

    halves = []
    for across in (1, 0):
        halves.append(pl.pallas_call(
            functools.partial(pair_kernel, across), out_shape=shaped((n_sta // 2, ROWS, 4 * share), f32),
            in_specs=[SMEM] * 2 + [VMEM] * 3 + [ANY] * len(halves), out_specs=VMEM,
            scratch_shapes=[pltpu.VMEM((4 * share, 384), f32)],
            compiler_params=PARAMS, name="pairs", cost_estimate=cost,
        )(first, second, left, right, back_table, *halves))
    hop = lambda v, dz, dh: lax.ppermute(v, STA, [(k, target(k, dz, dh, n_sta)) for k in range(n_sta)])
    slots = pl.pallas_call(
        add_kernel, out_shape=shaped((2 * n_sta, TALL, 2 * share), f32), in_specs=[VMEM] * 2, out_specs=VMEM,
        compiler_params=SMALL, name="add",
    )(hop(halves[0], 0, 1), halves[1])
    slots = lax.all_to_all(slots, ("z", "xl", "core"), 0, 0)
    out = pl.pallas_call(
        final_kernel, out_shape=shaped((1, steps, share, LAGS), f32),
        in_specs=[SMEM, VMEM], out_specs=VMEM, compiler_params=SMALL, name="finish",
    )(neighbours, slots)
    return out.transpose(0, 1, 3, 2)


def solution(mesh):
    fine = jax.sharding.Mesh(mesh.devices.reshape(4, 2, 2, 4, 2), CLU + STA)
    placed = (
        P(CLU, STA, None),
        P(),
        P(CLU, None),
        P(CLU, None, None),
        P(CLU, None, None),
    )
    return jax.shard_map(
        local, mesh=fine, in_specs=placed, out_specs=P(CLU, None, None, STA), check_vma=False
    )
```

```python
import functools
import math

import jax
import jax.numpy as jnp
import numpy as np
from jax import lax
from jax.experimental import pallas as pl
from jax.experimental.pallas import tpu as pltpu
from jax.sharding import PartitionSpec as P

CH, SAMP, HALF, LAGS = 48, 256, 32, 65
CLU, STA = ("y", "xl", "core"), ("z", "xh")
N = 288
LO, EXTRA = 128, 17
ROWS = 72
TALL = 40
EI, EJ = 68, 69


def tables():
    u = np.arange(SAMP)[:, None]
    k = np.arange(N // 2 + 1)[None, :]
    angle = 2 * math.pi * ((u * k) % N) / N
    c, s = np.cos(angle), np.sin(angle)
    ch, sh = c[:, LO:], s[:, LO:]
    pad = np.zeros((SAMP, 128 - 4 * EXTRA))
    left = np.concatenate([c[:, :LO], s[:, :LO], ch, sh, sh, ch, pad], axis=1)
    right = np.concatenate([c[:, :LO], s[:, :LO], ch, sh, ch, sh, pad], axis=1)
    lag = np.arange(LAGS)[:, None] - HALF
    angle = 2 * math.pi * ((lag * k) % N) / N
    weight = np.where((k == 0) | (k == N // 2), 1.0, 2.0) / N
    c, s = np.cos(angle) * weight, np.sin(angle) * weight
    back = np.zeros((ROWS, 384))
    back[:LAGS, :LO] = c[:, :LO]
    back[:LAGS, LO:2 * LO] = -s[:, :LO]
    ch, sh = c[:, LO:], s[:, LO:]
    back[:LAGS, 256:256 + 4 * EXTRA] = np.concatenate([ch, ch, -sh, sh], axis=1)
    back[LAGS, 256 + EI] = 1.0
    back[LAGS + 1, 256 + EJ] = 1.0

    def split(t, axis):
        t = t.astype(np.float32)
        hi = t.astype(jnp.bfloat16)
        lo = (t - hi.astype(np.float32)).astype(jnp.bfloat16)
        return np.concatenate([hi, lo], axis=axis)

    return split(left, 1), split(right, 1), split(back, 0)


def spectrum(x, table, energy_lane, one_lane):
    d = jnp.dot(x, table, preferred_element_type=jnp.float32)
    d = d[:, :384] + d[:, 384:]
    xf = x.astype(jnp.float32)
    energy = jnp.sum(xf * xf, axis=1, keepdims=True)
    lane = lax.broadcasted_iota(jnp.int32, (1, 128), 1)
    third = jnp.where(lane == energy_lane, energy, d[:, 256:])
    third = jnp.where(lane == one_lane, 1.0, third)
    return d[:, :128], d[:, 128:256], third


def place():
    x, core = lax.axis_index("xl"), lax.axis_index("core")
    return lax.axis_index("y"), x * 2 + core, x, core


def pack_kernel(rows_ref, cube_ref, local_ref, remote_ref, *refs):
    parts, (own_ref, core_ref, chip_ref, lists_ref, sems) = refs[:4], refs[4:]
    row, step, _, _ = place()
    quarter = parts[0].shape[0]
    cuts = [
        pltpu.make_async_copy(rows_ref.at[pl.ds(pl.multiple_of(((row + d) & 3) * quarter, quarter), quarter)], out, sems.at[d])
        for d, out in enumerate(parts)
    ]
    channels, _, width = cube_ref.shape
    size = cube_ref.shape[1] // 4
    outs = (own_ref, core_ref, chip_ref.at[0], chip_ref.at[1])
    first = [pltpu.make_async_copy(ref.at[0], lists_ref.at[n], sems.at[4 + n]) for n, ref in enumerate((local_ref, remote_ref))]
    copies = []
    for d, out in enumerate(outs):
        at = pl.multiple_of((step ^ d) * size, size)
        for c in range(channels):
            copies.append(pltpu.make_async_copy(
                cube_ref.at[c, pl.ds(at, size)], out.at[pl.ds(c * size, size)], sems.at[6 + d * channels + c]
            ))
    for copy in first + cuts + copies:
        copy.start()
    for copy in first:
        copy.wait()
    line = lax.broadcasted_iota(jnp.int32, (16, width), 0)
    for d, out in enumerate(outs):
        lists = jnp.zeros((16, width), jnp.float32)
        for n in range(2):
            listed = lists_ref[n, pl.ds(step ^ d, 1), :].astype(jnp.float32)
            per = listed.shape[1] // width
            for k in range(per):
                lists = jnp.where(line == n * per + k, listed[:, k * width:(k + 1) * width], lists)
        out[pl.ds(channels * size, 16), :] = lists.astype(jnp.bfloat16)
    for copy in cuts + copies:
        copy.wait()


def pick_kernel(owners_ref, g0, g1, g2, g3, give_ref):
    row, step, _, _ = place()
    for d in (1, 3):
        behind = (row + 4 - (owners_ref[step ^ d] >> 2)) & 3
        for n, ref in enumerate((g0, g1, g2, g3)):

            @pl.when(behind == n)
            def _():
                give_ref[d // 2] = ref[...]


def core_kernel(owners_ref, g0, g1, g2, g3, got_ref, _, mine_0, mine_1, theirs_0, theirs_1):
    row, step, _, core = place()
    size = mine_0.shape[0]
    for d, outs in ((0, (mine_0, mine_1)), (2, (theirs_0, theirs_1))):
        owner = owners_ref[step ^ d]
        here = (owner & 1) == core
        behind = jnp.where(here, (row + 4 - (owner >> 2)) & 3, 4)
        for n, ref in enumerate((g0, g1, g2, g3, got_ref.at[d // 2])):

            @pl.when(behind == n)
            def _():
                for k, to in enumerate(outs):
                    to[...] = ref[pl.ds(k * size, size), :]


def chip_kernel(owners_ref, mine_ref, got_ref, out_ref):
    _, step, x, _ = place()
    here = ((owners_ref[step] >> 1) & 1) == x

    @pl.when(here)
    def _():
        out_ref[...] = mine_ref[...]

    @pl.when(jnp.logical_not(here))
    def _():
        out_ref[...] = got_ref[...]


def clear_rest(out_ref, channels):
    events = out_ref.shape[0] // 24
    for k in range(3):
        for c in range(channels, 8):
            out_ref[pl.ds(k * 8 + c, events, stride=24), :] = jnp.zeros((events, 128), jnp.float32)


def left_kernel(table_ref, b0, b1, b2, b3, out_ref):
    events = out_ref.shape[0] // 24 // 4
    channels = b0.shape[0] // events
    clear_rest(out_ref, channels)
    for q, w_ref in enumerate((b0, b1, b2, b3)):
        parts = spectrum(w_ref[:channels * events], table_ref[...], EI, EJ)
        for c in range(channels):
            for n, part in enumerate(parts):
                to = pl.ds(q * events * 24 + n * 8 + c, events, stride=24)
                out_ref[to, :] = part[c * events:(c + 1) * events]


def right_kernel(table_ref, *refs):
    pieces, out_ref = refs[:-1], refs[-1]
    events = out_ref.shape[0] // 24
    size = pieces[0].shape[0]
    clear_rest(out_ref, len(pieces) * size // events)
    row = place()[0]
    for n, p_ref in enumerate(pieces):
        base = (((row + 4 - (0, 1, 3, 2)[n % 4]) & 3) * 2 + n // 4) * size
        x = p_ref[...]
        parts = spectrum(x, table_ref[...], EJ, EI)
        for g in range(x.shape[0] // 32):
            at = base + 32 * g
            c = at // events
            to = (at - c * events) * 24 + c
            for k, part in enumerate(parts):
                out_ref[pl.ds(to + 8 * k, 32, stride=24), :] = part[32 * g:32 * g + 32]


def channel_sum(vs, sub):
    for shift in (4, 2, 1):
        keep = (sub & shift) == 0
        half = len(vs) // 2
        couples = list(zip(vs[:half], vs[half:]))
        if shift == 4:
            vs = [jnp.where(keep, a, b) + pltpu.roll(jnp.where(keep, b, a), 4, 0) for a, b in couples]
        else:
            vs = [jnp.where(keep, a + pltpu.roll(a, 8 - shift, 0), b + pltpu.roll(b, shift, 0)) for a, b in couples]
    return vs[0]


MOVES = (2, 1, 3, 0)


def target(k, dz, dh, count):
    return ((k // 2 + dz) % (count // 2)) * 2 + (k % 2 + dh) % 2


def pair_kernel(across, local_ref, remote_ref, left, right, back_ref, *refs):
    out_ref, z = refs[-2:]
    width = out_ref.shape[2]
    half = out_ref.shape[0]
    sta = lax.axis_index(STA)
    share = width // 4
    pairs = local_ref.shape[0] // 4
    back = back_ref[...]
    contract = (((1,), (1,)), ((), ()))
    dot = lambda a, b: lax.dot_general(a, b, contract, preferred_element_type=jnp.float32)
    sub = lax.broadcasted_iota(jnp.int32, (8, 128), 0)
    for t in range(half):
        first = target(sta, MOVES[t], across, 2 * half) * share

        def body(it, carry):
            sums = []
            for part in range(8):
                g = it * 8 + part
                q = g >> 3
                at = q * pairs + first + (g & 7) * 8
                products = [[], [], []]
                for p in range(8):
                    i = pl.multiple_of(local_ref[at + p], 8)
                    j = pl.multiple_of(remote_ref[at + p], 8)
                    xa, xb, xc = left[pl.ds(i, 8)], left[pl.ds(i + 8, 8)], left[pl.ds(i + 16, 8)]
                    ya, yb, yc = right[pl.ds(j, 8)], right[pl.ds(j + 8, 8)], right[pl.ds(j + 16, 8)]
                    for col, v in enumerate((xa * ya + xb * yb, xb * ya - xa * yb, xc * yc)):
                        products[col].append(v)
                sums += [(g, col, channel_sum(products[col], sub)) for col in range(3)]
            for g, col, v in sums:
                z[pl.ds(pl.multiple_of(g * 8, 8), 8), col * 128:col * 128 + 128] = v
            return carry

        lax.fori_loop(0, width // 64, body, 0)
        zk = z[...]
        zh = zk.astype(jnp.bfloat16)
        zl = (zk - zh.astype(jnp.float32)).astype(jnp.bfloat16)
        high = dot(back, zh)
        out_ref[t] = high[:ROWS] + high[ROWS:] + dot(back[:ROWS], zl)


def add_kernel(a_ref, b_ref, out_ref):
    z, step = lax.axis_index("z"), place()[1]
    share = a_ref.shape[2] // 4
    for t, dz in enumerate(MOVES):
        total = a_ref[t] + b_ref[t]
        for q in range(4):
            part = total[:, q * share:(q + 1) * share]
            slot = ((z + dz) & 3) * 4 + (step ^ q)
            out_ref[slot, :, :share] = part[:TALL]
            out_ref[slot, :ROWS - TALL, share:] = part[TALL:]


def final_kernel(near_ref, got_ref, out_ref):
    share = out_ref.shape[2]
    count = CH * SAMP
    for s in range(4):
        total = (got_ref[s] + got_ref[4 + s]) + (got_ref[8 + s] + got_ref[12 + s])
        total = jnp.concatenate([total[:, :share], total[:ROWS - TALL, share:]], axis=0)
        ni = 1.0 / jnp.sqrt(total[LAGS:LAGS + 1] / count + 1e-6)
        nj = 1.0 / jnp.sqrt(total[LAGS + 1:LAGS + 2] / count + 1e-6)
        out_ref[0, s] = (total * (ni * nj / count * near_ref[0, s].astype(jnp.float32))).T[:, :LAGS]


HBM = pl.BlockSpec(memory_space=pltpu.HBM)
ANY = pl.BlockSpec(memory_space=pl.ANY)
SMEM = pl.BlockSpec(memory_space=pltpu.SMEM)
VMEM = pl.BlockSpec(memory_space=pltpu.VMEM)
PARAMS = pltpu.CompilerParams(vmem_limit_bytes=20 * 1024 * 1024)
SMALL = pltpu.CompilerParams(vmem_limit_bytes=8 * 1024 * 1024)


def in_hbm(v):
    return pltpu.with_memory_space_constraint(v, pltpu.HBM)


def local(waves, owners, neighbours, pair_local, pair_remote):
    ev, ch, samp = waves.shape
    steps = owners.shape[0]
    pairs = pair_local.shape[2]
    n_clu, n_sta = lax.axis_size(CLU), lax.axis_size(STA)
    share = pairs // n_sta
    block = ev // steps
    left_table, right_table, back_table = (jnp.asarray(t) for t in tables())
    cube = waves.transpose(1, 0, 2)
    rows = cube.reshape(ch * ev, samp)
    f32, bf16 = jnp.float32, jnp.bfloat16
    shaped = jax.ShapeDtypeStruct

    me = lax.axis_index(CLU)
    row, step = me // 4, me % 4
    near = lambda v, d: v if d == 0 else lax.ppermute(v, CLU, [(i, i ^ d) for i in range(n_clu)])
    turn = lambda v, d: lax.ppermute(v, CLU, [(i, (i + 4 * d) % n_clu) for i in range(n_clu)])

    quarter = ch * ev // 4
    piece = shaped((quarter, samp), bf16)
    height = ch * block + 16
    payload = shaped((height, samp), bf16)
    *parts, own, core, chip = pl.pallas_call(
        pack_kernel, out_shape=(piece,) * 4 + (payload, payload, shaped((2, height, samp), bf16)),
        in_specs=[HBM] * 4, out_specs=(VMEM,) * 7,
        scratch_shapes=[pltpu.VMEM((2, steps, pairs), jnp.int32), pltpu.SemaphoreType.DMA((6 + 4 * ch,))],
        compiler_params=SMALL, name="pack",
    )(in_hbm(rows), in_hbm(cube), in_hbm(pair_local), in_hbm(pair_remote))
    chip = near(chip, 2)
    blocks = [own, near(core, 1), chip[0], near(chip[1], 1)]
    got = [part if d == 0 else turn(part, d) for d, part in enumerate(parts)]
    give = pl.pallas_call(
        pick_kernel, out_shape=shaped((2, quarter, samp), bf16), in_specs=[SMEM] + [VMEM] * 4, out_specs=VMEM,
        compiler_params=SMALL, name="pick",
    )(in_hbm(owners), *got)
    part = shaped((quarter // 2, samp), bf16)
    *mine, theirs_0, theirs_1 = pl.pallas_call(
        core_kernel, out_shape=(part,) * 4, in_specs=[SMEM] + [VMEM] * 5 + [ANY], out_specs=(VMEM,) * 4,
        compiler_params=SMALL, name="over_core",
    )(owners, *got, near(give, 1), chip)
    pieces = []
    for kept, sent in zip(mine, [near(theirs_0, 2), near(theirs_1, 2)]):
        whole = pl.pallas_call(
            chip_kernel, out_shape=part, in_specs=[SMEM] + [VMEM] * 2, out_specs=VMEM,
            compiler_params=SMALL, name="over_x",
        )(owners, kept, sent)
        pieces += [whole] + [turn(whole, d) for d in (1, -1, 2)]

    listed = jnp.stack([b[ch * block:ch * block + 2 * pairs // samp] for b in blocks]).astype(jnp.int32)
    listed = listed.reshape(4, 2, pairs) * 24
    first = listed[:, 0] + jnp.arange(4, dtype=jnp.int32)[:, None] * (block * 24)
    first, second = first.reshape(4 * pairs), listed[:, 1].reshape(4 * pairs)

    spectra = shaped((ev * 24, 128), f32)
    cost = pl.CostEstimate(flops=2 * ch * ev * samp * 768, bytes_accessed=4000000, transcendentals=0)
    left = pl.pallas_call(
        left_kernel, out_shape=spectra, in_specs=[VMEM] * 5, out_specs=VMEM,
        compiler_params=PARAMS, name="left", cost_estimate=cost,
    )(left_table, *blocks)
    right = pl.pallas_call(
        right_kernel, out_shape=spectra, in_specs=[VMEM] * (1 + len(pieces)), out_specs=VMEM,
        compiler_params=PARAMS, name="right", cost_estimate=cost,
    )(right_table, *pieces)

    halves = []
    for across in (1, 0):
        halves.append(pl.pallas_call(
            functools.partial(pair_kernel, across), out_shape=shaped((n_sta // 2, ROWS, 4 * share), f32),
            in_specs=[SMEM] * 2 + [VMEM] * 3 + [ANY] * len(halves), out_specs=VMEM,
            scratch_shapes=[pltpu.VMEM((4 * share, 384), f32)],
            compiler_params=PARAMS, name="pairs", cost_estimate=cost,
        )(first, second, left, right, back_table, *halves))
    hop = lambda v, dz, dh: lax.ppermute(v, STA, [(k, target(k, dz, dh, n_sta)) for k in range(n_sta)])
    slots = pl.pallas_call(
        add_kernel, out_shape=shaped((2 * n_sta, TALL, 2 * share), f32), in_specs=[VMEM] * 2, out_specs=VMEM,
        compiler_params=SMALL, name="add",
    )(hop(halves[0], 0, 1), halves[1])
    slots = lax.all_to_all(slots, ("z", "xl", "core"), 0, 0)
    out = pl.pallas_call(
        final_kernel, out_shape=shaped((1, steps, share, LAGS), f32),
        in_specs=[SMEM, VMEM], out_specs=VMEM, compiler_params=SMALL, name="finish",
    )(neighbours, slots)
    return out.transpose(0, 1, 3, 2)


def solution(mesh):
    fine = jax.sharding.Mesh(mesh.devices.reshape(4, 2, 2, 4, 2), CLU + STA)
    placed = (
        P(CLU, STA, None),
        P(),
        P(CLU, None),
        P(CLU, None, None),
        P(CLU, None, None),
    )
    return jax.shard_map(
        local, mesh=fine, in_specs=placed, out_specs=P(CLU, None, None, STA), check_vma=False
    )
```
